32 devices in a mesh: pole: 2 (over x), row: 8 (over z, y), col: 2 (over core).
Axes of the slice: x: 2, y: 2, z: 4, core: 2. Of those that a mesh axis runs over, the one named last changes fastest.
Arguments:
- inverse: float32 [16, 2, 256, 256], P(('pole', 'row'), 'col'), parts along dimension 0, as said below
- panel: float32 [16, 2, 64, 1024], P(('pole', 'row'), 'col'), parts along dimension 0, may hold values from -0.25 to 0.25
- pattern: int32 [4, 4], replicated, may hold values 0 or 1
- dinv: float32 [8, 256, 256], P('pole', 'row', 'col'), parts along dimension 0, may hold values from -6 to 6
Outputs:
- off_diagonal: float32 [16, 2, 64, 1024], P(('pole', 'row'), 'col'), parts along dimension 0
- diagonal: float32 [8, 256, 256], P('pole', 'row', 'col'), parts along dimension 0
The draws below stay inside these ranges and needn't reach their ends.
There are 2 independent parts, one for each index of `pole`. The reference program is written for one: setup_inputs(seed, part) draws one part's arguments, and reference() takes and returns one part's arrays. A program takes and returns all parts, laid end to end along the dimension named above; an argument that names none is the same for every part. Nothing has to cross between parts.
Inputs may be any that keep to these rules, and one draw needn't show every extreme that they name: inverse, read as the 1024 x 1024 matrix A of the first step, is symmetric.
All inputs are finite; a program needn't handle non-finite values.
Results may differ from the reference program's by a relative error of at most 0.000078.
Values sent between devices are 32-bit elements; how exact they have to be, the bound alone decides.
A program may use at most 64 MiB of HBM per device.

```python
import jax
import jax.numpy as jnp
from jax import lax

W = 256
NSUP = 4
ROWS_DEV = 64
NCOLS = 1024
M = 1024
GR = 4
GC = 4
RB = 256
CB = 256
NB = 4
N_ROW = 8
N_COL = 2


def draw_inverse(key, part):
    key = jax.random.fold_in(key, 11)
    first_key = jax.random.fold_in(key, 0)
    base = jax.random.normal(first_key, (M, M), jnp.float32)
    symmetric = (base + base.T) * 0.70710678
    return symmetric.reshape(GR, RB, GC, CB).transpose(0, 2, 1, 3).reshape(N_ROW, N_COL, RB, CB)


def place_ends(array, own_key, smallest, high):
    place = [jax.random.randint(jax.random.fold_in(own_key, axis), (), 0, length) for axis, length in enumerate(array.shape)]
    main_axis = array.shape.index(max(array.shape))
    neighbour = place[:main_axis] + [(place[main_axis] + 1) % array.shape[main_axis]] + place[main_axis + 1:]
    return array.at[tuple(place)].set(smallest).at[tuple(neighbour)].set(high)


def steps_of(key, dims, cuts, smallest, largest):
    factor_of = 1.0
    for position, shards_of in cuts:
        steps = jax.random.uniform(jax.random.fold_in(jax.random.fold_in(key, 6), position), (shards_of,), jnp.float32, smallest / len(cuts), largest / len(cuts))
        factor_of = factor_of * jnp.repeat(jnp.exp(steps), dims[position] // shards_of).reshape((-1,) + (1,) * (len(dims) - 1 - position))
    return factor_of


def bell_draw(key, shape, spread, bound, pieces=(), kind=jnp.bfloat16):
    result = spread * jax.random.normal(key, shape, jnp.float32)
    if pieces:
        result = result * steps_of(key, shape, pieces, -0.22, 0.18)
    return jnp.clip(result, -bound, bound).astype(kind)


def setup_inputs(seed: int = 0, part: int = 0) -> dict:
    key_list = jax.random.split(jax.random.key(seed), 5)
    part_splits = jax.random.split(jax.random.fold_in(key_list[4], part), 5)
    return {
        "inverse": draw_inverse(jax.random.fold_in(jax.random.fold_in(key_list[4], part), 71), part),
        "panel": bell_draw(part_splits[1], (N_ROW, N_COL, ROWS_DEV, NCOLS), (M // 2) ** -0.5, 0.25, ((0, 8), (1, 2)), jnp.float32),
        "pattern": place_ends((jax.random.randint(key_list[2], (NB, NSUP), 0, 2) < 1).astype(jnp.int32), jax.random.fold_in(key_list[2], 1), 0, 1),
        "dinv": bell_draw(part_splits[3], (NSUP, W, W), 1.0, 6.0, ((1, 8), (2, 2)), jnp.float32),
    }


def reference(inverse, panel, pattern, dinv):
    full_inverse = inverse.reshape(GR, GC, RB, CB).transpose(0, 2, 1, 3).reshape(M, M)
    panel_rows = panel.reshape(GR, GC, ROWS_DEV, NCOLS).transpose(1, 0, 2, 3).reshape(M, NCOLS)
    row_blocks = jnp.arange(M, dtype=jnp.int32) // W
    col_blocks = jnp.arange(NCOLS, dtype=jnp.int32) // W
    keep = pattern[row_blocks][:, col_blocks].astype(jnp.float32)
    lhat = panel_rows * keep
    product = jnp.dot(full_inverse, lhat, precision=lax.Precision.HIGHEST, preferred_element_type=jnp.float32)
    masked = -(product * keep)
    off_diagonal = masked.reshape(GC, GR, ROWS_DEV, NCOLS).transpose(1, 0, 2, 3).reshape(N_ROW, N_COL, ROWS_DEV, NCOLS)
    diag_terms = jnp.einsum("gkw,gkv->kwv", lhat.reshape(M, NSUP, W), product.reshape(M, NSUP, W),
                            precision=lax.Precision.HIGHEST)
    return off_diagonal, dinv + diag_terms
```

```python
import jax
import jax.numpy as jnp
from jax import lax
from jax.experimental import pallas as pl
from jax.experimental.pallas import tpu as pltpu
from jax.sharding import PartitionSpec as P


def swapped(value, axis, apart):
    mask = 2**apart
    pairs = [(source, source ^ mask) for source in range(lax.axis_size(axis))]
    return lax.ppermute(value, axis, pairs)


def group_flip(current, position, col_bits):
    if position < col_bits:
        return swapped(current, "col", position)
    return swapped(current, "row", position - col_bits)


def cross_flip(current, position, col_bits):
    if position < col_bits:
        return swapped(current, "col", position)
    return swapped(current, "row", position - col_bits)


def bit_at(device_at, position):
    return device_at >> position & 1


def collect(current, positions, device_at, col_bits):
    for position in positions:
        partner = group_flip(current, position, col_bits)
        upper_half = bit_at(device_at, position) == 1
        current = jnp.where(
            upper_half,
            jnp.concatenate([partner, current], 0),
            jnp.concatenate([current, partner], 0),
        )
    return current


def reduce_split(current, positions, device_at, col_bits):
    for position in positions:
        halfway = current.shape[0] // 2
        mine_bit = bit_at(device_at, position)
        kept_half = lax.dynamic_slice_in_dim(current, mine_bit * halfway, halfway, 0)
        sent_half = lax.dynamic_slice_in_dim(current, (1 - mine_bit) * halfway, halfway, 0)
        current = kept_half + group_flip(sent_half, position, col_bits)
    return current


def relabel(current, targets, device_at, col_bits):
    mapping = list(range(len(targets)))
    for column in range(len(targets)):
        if mapping[column] != targets[column]:
            lead_bit = mapping[column]
            other_bit = targets[column]
            shifted = cross_flip(cross_flip(current, lead_bit, col_bits), other_bit, col_bits)
            unequal = bit_at(device_at, lead_bit) != bit_at(device_at, other_bit)
            current = jnp.where(unequal, shifted, current)
            mapping = [
                other_bit if element == lead_bit else lead_bit if element == other_bit else element
                for element in mapping
            ]
    return current


def general_body(inverse, panel, pattern, dinv):
    n_row = lax.axis_size("row")
    n_col = lax.axis_size("col")
    device_at = lax.axis_index("row") * n_col + lax.axis_index("col")
    grid_rows = min(8, n_row // 2)
    grid_cols = n_row * n_col // grid_rows
    col_bits = n_col.bit_length() - 1
    total_bits = (n_row * n_col).bit_length() - 1
    high_bits = grid_rows.bit_length() - 1
    side_bits = total_bits - high_bits
    grid_row = device_at // grid_cols
    grid_col = device_at % grid_cols
    rows_dev, col_count = (panel.shape[2], panel.shape[3])
    nblocks, sup_count = pattern.shape
    sup_width = col_count // sup_count
    first_row = (grid_col * grid_rows + grid_row) * rows_dev
    global_rows = first_row + jnp.arange(rows_dev, dtype=jnp.int32)
    onehot = (
        global_rows[:, None] // sup_width == jnp.arange(nblocks, dtype=jnp.int32)[None, :]
    ).astype(jnp.float32)
    keep_sup = jnp.dot(onehot, pattern.astype(jnp.float32), precision=lax.Precision.HIGHEST)
    keep_piece = jnp.broadcast_to(keep_sup[:, :, None], (rows_dev, sup_count, sup_width)).reshape(
        rows_dev, col_count
    )
    lhat_piece = panel.reshape(rows_dev, col_count) * keep_piece
    inverse_block = inverse.reshape(inverse.shape[2], inverse.shape[3])
    gathered = collect(lhat_piece, list(range(side_bits, total_bits)), device_at, col_bits)
    partial_sum = jnp.dot(
        inverse_block, gathered, precision=lax.Precision.HIGHEST, preferred_element_type=jnp.float32
    )
    row_piece = reduce_split(partial_sum, list(range(side_bits - 1, -1, -1)), device_at, col_bits)
    backward = [(bit_slot + side_bits) % total_bits for bit_slot in range(total_bits)]
    product_piece = relabel(row_piece, backward, device_at, col_bits)
    diag_terms = jnp.einsum(
        "rkw,rkv->kwv",
        lhat_piece.reshape(rows_dev, sup_count, sup_width),
        product_piece.reshape(rows_dev, sup_count, sup_width),
        precision=lax.Precision.HIGHEST,
    )
    arranged = diag_terms.reshape(sup_count, n_row, sup_width // n_row, n_col, sup_width // n_col)
    arranged = arranged.transpose(1, 3, 0, 2, 4).reshape(
        n_row * n_col, sup_count, sup_width // n_row, sup_width // n_col
    )
    diagonal = dinv + lax.psum_scatter(arranged, ("row", "col"), scatter_dimension=0, tiled=True)[0]
    off_diagonal = (-(product_piece * keep_piece)).reshape(panel.shape)
    return (off_diagonal, diagonal)


MESH = pl.DeviceIdType.MESH
HIGHEST = lax.Precision.HIGHEST
GRID = 4

ROUTES = {
    (0, 0): ([(1, 0, 0)], [], [(1, 0, 2)], [(1, 0, 3)]),
    (0, 1): ([(0, 0, 1)], [], [(0, 2, 1)], [(0, 3, 1)]),
    (0, 2): ([(0, 0, 2)], [], [(0, 3, 2)], []),
    (0, 3): ([(0, 0, 3)], [], [], []),
    (1, 0): ([(1, 1, 0)], [(2, 0, 0)], [(1, 2, 0)], [(1, 3, 0)]),
    (1, 1): ([(0, 1, 1), (2, 1, 1)], [(2, 1, 0)], [(0, 1, 2)], [(0, 1, 3)]),
    (1, 2): ([(1, 1, 2)], [(0, 2, 2)], [(0, 2, 3), (1, 3, 2)], []),
    (1, 3): ([(1, 1, 3)], [(0, 3, 3)], [], []),
}


def numbered(routes):
    count = 0
    out = []
    for targets in routes:
        out.append([(count + n,) + t for n, t in enumerate(targets)])
        count += len(targets)
    return out


def kernel(pattern_ref, a_ref, p_ref, dinv_ref, off_ref, diag_ref,
           abuf, pbuf, acc, stage, dpart, dbuf, ebuf, dfin,
           a_send, a_recv, p_send, p_recv, f_send, g_send, o_send, o_recv,
           d_send, d_recv, e_send, e_recv):
    width = a_ref.shape[0]
    sub = p_ref.shape[0]
    half_u, half_v = dinv_ref.shape[1], dinv_ref.shape[2]
    pole = lax.axis_index("pole")
    row = lax.axis_index("row")
    c = lax.axis_index("col")
    z = row // 2
    y = row % 2
    q = 2 * y + c
    mirror = z // 2

    def flip(v):
        return v + mirror * (GRID - 1 - 2 * v)

    zf, qf = flip(z), flip(q)

    def dev(zt, qt):
        return (pole, zt * 2 + qt // 2, qt % 2)

    def copy_to(src, dst, send, recv, where):
        return pltpu.make_async_remote_copy(
            src_ref=src, dst_ref=dst, send_sem=send, recv_sem=recv,
            device_id=where, device_id_type=MESH)

    barrier = pltpu.get_barrier_semaphore()
    me = z * GRID + q
    for d in range(1, GRID * GRID):
        other = (me + d) % (GRID * GRID)
        pl.semaphore_signal(barrier, inc=1, device_id=dev(other // GRID, other % GRID), device_id_type=MESH)
    pl.semaphore_wait(barrier, GRID * GRID - 1)

    core_mate = q + 1 - 2 * c
    across = q + 2 - 4 * y

    def cols(k):
        return pl.ds(pl.multiple_of(k * width, width), width)

    def part(block, r):
        return pl.ds(pl.multiple_of(block * width + r * sub, sub), sub)

    z_copies = []
    for d in (1, 3, 2):
        zt = (z + d) % GRID
        cp = copy_to(p_ref.at[:, cols(zt)], pbuf.at[part(q, z), :], p_send.at[d], p_recv.at[q * GRID + z], dev(zt, q))
        cp.start()
        z_copies.append(cp)

    def a_copy(src, n, tz, tq, slot):
        return copy_to(src, abuf.at[flip(slot)], a_send.at[n], a_recv.at[flip(slot)], dev(flip(tz), flip(tq)))

    def a_pass(step, src):
        for (cz, cq), routes in ROUTES.items():
            targets = numbered(routes)[step]
            if targets:
                @pl.when((zf == cz) & (qf == cq))
                def _():
                    for n, tz, tq, slot in targets:
                        a_copy(src, n, tz, tq, slot).start()

    a_pass(0, a_ref)

    upper, odd = qf // 2, qf % 2
    away = 1 - zf
    slots = (
        flip((1 - upper) * away + upper * qf),
        flip((1 - upper) * 2 + upper * ((1 - odd) * 3 + odd * away)),
        flip((1 - upper) * 3 + upper * ((1 - odd) * away + odd * 2)),
    )

    def a_arrive(step):
        slot = slots[step]
        pltpu.make_async_copy(abuf.at[slot], abuf.at[slot], a_recv.at[slot]).wait()
        a_pass(step + 1, abuf.at[slot])

    def p_wait(block, r):
        ref = pbuf.at[part(block, r), :]
        pltpu.make_async_copy(ref, ref, p_recv.at[block * GRID + r]).wait()

    layer_copies = []

    def p_share(src, r, d):
        for n, qt in ((0, across), (1, core_mate)):
            cp = copy_to(src, pbuf.at[part(q, r), :], f_send.at[2 * d + n], p_recv.at[q * GRID + r], dev(z, qt))
            cp.start()
            layer_copies.append(cp)

    p_share(p_ref.at[:, cols(z)], z, 0)
    pbuf[part(q, z), :] = p_ref[:, cols(z)]
    for d in (1, 3, 2):
        r = (z + d) % GRID
        p_wait(q, r)
        p_share(pbuf.at[part(q, r), :], r, d)
    a_arrive(0)
    for d in (0, 1, 3, 2):
        r = (z + d) % GRID
        p_wait(across, r)
        ref = pbuf.at[part(across, r), :]
        cp = copy_to(ref, ref, g_send.at[d], p_recv.at[across * GRID + r], dev(z, core_mate))
        cp.start()
        layer_copies.append(cp)
    for block in (core_mate, core_mate + 2 - 4 * y):
        for r in range(GRID):
            p_wait(block, r)

    def lhat(block):
        rows = pl.ds(pl.multiple_of(block * width, width), width)
        return pbuf[rows, :] * pattern_ref[block, z].astype(jnp.float32)

    def dot_t(left, right):
        return lax.dot_general(left, right, (((0,), (0,)), ((), ())), precision=HIGHEST,
                               preferred_element_type=jnp.float32)

    acc[...] = dot_t(a_ref[...], lhat(z))
    for step in range(3):
        if step:
            a_arrive(step)
        slot = slots[step]
        slot_f = flip(slot)
        turned = (qf != zf) & (qf >= 2) & (slot_f < qf)

        @pl.when(turned)
        def _():
            acc[...] += dot_t(abuf[slot], lhat(slot))

        @pl.when(jnp.logical_not(turned))
        def _():
            acc[...] += jnp.dot(abuf[slot], lhat(slot), precision=HIGHEST, preferred_element_type=jnp.float32)

    product = acc[...]
    stage[...] = -(product * pattern_ref[q, z].astype(jnp.float32))
    out_copies = []
    for d in (1, 3, 2):
        zt = (z + d) % GRID
        cp = copy_to(stage.at[part(0, zt), :], off_ref.at[:, cols(z)], o_send.at[d], o_recv.at[z], dev(zt, q))
        cp.start()
        out_copies.append(cp)
    dpart[...] = dot_t(lhat(q), product)
    for d in (2, 1, 3):
        qt = (q + d) % GRID
        cp = copy_to(dpart.at[part(0, qt), :], dbuf.at[d - 1], d_send.at[d], d_recv.at[d - 1], dev(z, qt))
        cp.start()
        out_copies.append(cp)
    off_ref[:, cols(z)] = stage[part(0, z), :]
    total = dpart[part(0, q), :]
    for d in (1, 2, 3):
        pltpu.make_async_copy(dbuf.at[d - 1], dbuf.at[d - 1], d_recv.at[d - 1]).wait()
        total = total + dbuf[d - 1]
    for qt in range(GRID):
        yt, ct = qt // 2, qt % 2
        ebuf[qt] = total[yt * half_u:(yt + 1) * half_u, ct * half_v:(ct + 1) * half_v]
    e_copies = [copy_to(ebuf.at[qt], dfin.at[z], e_send.at[qt], e_recv.at[z], dev(q, qt)) for qt in range(GRID)]
    for qt in range(GRID):
        own = (q == z) & (q == qt)

        @pl.when(jnp.logical_not(own))
        def _():
            e_copies[qt].start()

        @pl.when(own)
        def _():
            dfin[z] = ebuf[qt]

    for d in (1, 3, 2):
        zs = (z + d) % GRID
        ref = off_ref.at[:, cols(zs)]
        pltpu.make_async_copy(ref, ref, o_recv.at[zs]).wait()
    for k in range(GRID):
        @pl.when(jnp.logical_not((q == z) & (z == k)))
        def _():
            pltpu.make_async_copy(dfin.at[k], dfin.at[k], e_recv.at[k]).wait()
        diag_ref[k] = dinv_ref[k] + dfin[k]

    for cp in z_copies + layer_copies + out_copies:
        cp.wait_send()
    for qt in range(GRID):
        @pl.when(jnp.logical_not((q == z) & (q == qt)))
        def _():
            e_copies[qt].wait_send()
    for (cz, cq), routes in ROUTES.items():
        @pl.when((zf == cz) & (qf == cq))
        def _():
            for targets in numbered(routes):
                for n, tz, tq, slot in targets:
                    a_copy(a_ref, n, tz, tq, slot).wait_send()


def square_grid(inverse, panel, pattern, dinv):
    width = inverse.shape[3]
    sub, ncols = panel.shape[2], panel.shape[3]
    vmem = pl.BlockSpec(memory_space=pltpu.VMEM)
    dma = pltpu.SemaphoreType.DMA
    f32 = jnp.float32
    off, diagonal = pl.pallas_call(
        kernel,
        out_shape=(jax.ShapeDtypeStruct((sub, ncols), f32), jax.ShapeDtypeStruct(dinv.shape, f32)),
        in_specs=[pl.BlockSpec(memory_space=pltpu.SMEM), vmem, vmem, vmem],
        out_specs=(vmem, vmem),
        scratch_shapes=[
            pltpu.VMEM((GRID, width, width), f32),
            pltpu.VMEM((GRID * width, width), f32),
            pltpu.VMEM((width, width), f32),
            pltpu.VMEM((width, width), f32),
            pltpu.VMEM((width, width), f32),
            pltpu.VMEM((GRID - 1, sub, width), f32),
            pltpu.VMEM((GRID,) + dinv.shape[1:], f32),
            pltpu.VMEM(dinv.shape, f32),
            dma((8,)), dma((GRID,)), dma((GRID,)), dma((GRID * GRID,)), dma((2 * GRID,)), dma((GRID,)),
            dma((GRID,)), dma((GRID,)), dma((GRID,)), dma((GRID,)), dma((GRID,)), dma((GRID,)),
        ],
        compiler_params=pltpu.CompilerParams(
            collective_id=0, has_side_effects=True, vmem_limit_bytes=32 * 1024 * 1024),
    )(pattern, inverse.reshape(inverse.shape[2:]), panel.reshape(panel.shape[2:]), dinv)
    return off.reshape(panel.shape), diagonal


def fits_square_grid(mesh_shape, inverse, panel, pattern, dinv):
    n_row, n_col = mesh_shape["row"], mesh_shape["col"]
    width = inverse.shape[3]
    return (
        n_row == 2 * GRID and n_col == 2
        and inverse.shape[2] == width and width % 128 == 0
        and pattern.shape == (GRID, GRID)
        and panel.shape[2] * GRID == width and panel.shape[3] == GRID * width
        and dinv.shape == (GRID, width // n_row, width // n_col)
    )


def body(inverse, panel, pattern, dinv):
    sizes = {"row": lax.axis_size("row"), "col": lax.axis_size("col")}
    if fits_square_grid(sizes, inverse, panel, pattern, dinv):
        return square_grid(inverse, panel, pattern, dinv)
    return general_body(inverse, panel, pattern, dinv)


def solution(mesh):
    return jax.shard_map(
        body,
        mesh=mesh,
        in_specs=(
            P(("pole", "row"), "col", None, None),
            P(("pole", "row"), "col", None, None),
            P(),
            P("pole", "row", "col"),
        ),
        out_specs=(P(("pole", "row"), "col", None, None), P("pole", "row", "col")),
        check_vma=False,
    )
```

```python
import jax
import jax.numpy as jnp
from jax import lax
from jax.experimental import pallas as pl
from jax.experimental.pallas import tpu as pltpu
from jax.sharding import PartitionSpec as P


def swapped(value, axis, apart):
    mask = 2**apart
    pairs = [(source, source ^ mask) for source in range(lax.axis_size(axis))]
    return lax.ppermute(value, axis, pairs)


def group_flip(current, position, col_bits):
    if position < col_bits:
        return swapped(current, "col", position)
    return swapped(current, "row", position - col_bits)


def cross_flip(current, position, col_bits):
    if position < col_bits:
        return swapped(current, "col", position)
    return swapped(current, "row", position - col_bits)


def bit_at(device_at, position):
    return device_at >> position & 1


def collect(current, positions, device_at, col_bits):
    for position in positions:
        partner = group_flip(current, position, col_bits)
        upper_half = bit_at(device_at, position) == 1
        current = jnp.where(
            upper_half,
            jnp.concatenate([partner, current], 0),
            jnp.concatenate([current, partner], 0),
        )
    return current


def reduce_split(current, positions, device_at, col_bits):
    for position in positions:
        halfway = current.shape[0] // 2
        mine_bit = bit_at(device_at, position)
        kept_half = lax.dynamic_slice_in_dim(current, mine_bit * halfway, halfway, 0)
        sent_half = lax.dynamic_slice_in_dim(current, (1 - mine_bit) * halfway, halfway, 0)
        current = kept_half + group_flip(sent_half, position, col_bits)
    return current


def relabel(current, targets, device_at, col_bits):
    mapping = list(range(len(targets)))
    for column in range(len(targets)):
        if mapping[column] != targets[column]:
            lead_bit = mapping[column]
            other_bit = targets[column]
            shifted = cross_flip(cross_flip(current, lead_bit, col_bits), other_bit, col_bits)
            unequal = bit_at(device_at, lead_bit) != bit_at(device_at, other_bit)
            current = jnp.where(unequal, shifted, current)
            mapping = [
                other_bit if element == lead_bit else lead_bit if element == other_bit else element
                for element in mapping
            ]
    return current


def general_body(inverse, panel, pattern, dinv):
    n_row = lax.axis_size("row")
    n_col = lax.axis_size("col")
    device_at = lax.axis_index("row") * n_col + lax.axis_index("col")
    grid_rows = min(8, n_row // 2)
    grid_cols = n_row * n_col // grid_rows
    col_bits = n_col.bit_length() - 1
    total_bits = (n_row * n_col).bit_length() - 1
    high_bits = grid_rows.bit_length() - 1
    side_bits = total_bits - high_bits
    grid_row = device_at // grid_cols
    grid_col = device_at % grid_cols
    rows_dev, col_count = (panel.shape[2], panel.shape[3])
    nblocks, sup_count = pattern.shape
    sup_width = col_count // sup_count
    first_row = (grid_col * grid_rows + grid_row) * rows_dev
    global_rows = first_row + jnp.arange(rows_dev, dtype=jnp.int32)
    onehot = (
        global_rows[:, None] // sup_width == jnp.arange(nblocks, dtype=jnp.int32)[None, :]
    ).astype(jnp.float32)
    keep_sup = jnp.dot(onehot, pattern.astype(jnp.float32), precision=lax.Precision.HIGHEST)
    keep_piece = jnp.broadcast_to(keep_sup[:, :, None], (rows_dev, sup_count, sup_width)).reshape(
        rows_dev, col_count
    )
    lhat_piece = panel.reshape(rows_dev, col_count) * keep_piece
    inverse_block = inverse.reshape(inverse.shape[2], inverse.shape[3])
    gathered = collect(lhat_piece, list(range(side_bits, total_bits)), device_at, col_bits)
    partial_sum = jnp.dot(
        inverse_block, gathered, precision=lax.Precision.HIGHEST, preferred_element_type=jnp.float32
    )
    row_piece = reduce_split(partial_sum, list(range(side_bits - 1, -1, -1)), device_at, col_bits)
    backward = [(bit_slot + side_bits) % total_bits for bit_slot in range(total_bits)]
    product_piece = relabel(row_piece, backward, device_at, col_bits)
    diag_terms = jnp.einsum(
        "rkw,rkv->kwv",
        lhat_piece.reshape(rows_dev, sup_count, sup_width),
        product_piece.reshape(rows_dev, sup_count, sup_width),
        precision=lax.Precision.HIGHEST,
    )
    arranged = diag_terms.reshape(sup_count, n_row, sup_width // n_row, n_col, sup_width // n_col)
    arranged = arranged.transpose(1, 3, 0, 2, 4).reshape(
        n_row * n_col, sup_count, sup_width // n_row, sup_width // n_col
    )
    diagonal = dinv + lax.psum_scatter(arranged, ("row", "col"), scatter_dimension=0, tiled=True)[0]
    off_diagonal = (-(product_piece * keep_piece)).reshape(panel.shape)
    return (off_diagonal, diagonal)


MESH = pl.DeviceIdType.MESH
HIGHEST = lax.Precision.HIGHEST
GRID = 4
CHUNKS = 4

ROUTES = {
    (0, 0): ([(1, 0, 0)], [], [(1, 0, 2)], [(1, 0, 3)]),
    (0, 1): ([(0, 0, 1)], [], [(0, 2, 1)], [(0, 3, 1)]),
    (0, 2): ([(0, 0, 2)], [], [(0, 3, 2)], []),
    (0, 3): ([(0, 0, 3)], [], [], []),
    (1, 0): ([(1, 1, 0)], [(2, 0, 0)], [(1, 2, 0)], [(1, 3, 0)]),
    (1, 1): ([(0, 1, 1), (2, 1, 1)], [(2, 1, 0)], [(0, 1, 2)], [(0, 1, 3)]),
    (1, 2): ([(1, 1, 2)], [(0, 2, 2)], [(0, 2, 3), (1, 3, 2)], []),
    (1, 3): ([(1, 1, 3)], [(0, 3, 3)], [], []),
}


def numbered(routes):
    count = 0
    out = []
    for targets in routes:
        out.append([(count + n,) + t for n, t in enumerate(targets)])
        count += len(targets)
    return out


def kernel(pattern_hbm, a_hbm, p_hbm, dinv_hbm, off_ref, diag_ref,
           pattern_ref, a_ref, dinv_ref, l_sem, abuf, pbuf, acc, stage, dpart, dbuf, ebuf, dfin,
           a_send, a_recv, p_send, p_recv, f_send, g_send, o_send, o_recv,
           d_send, d_recv, e_send, e_recv):
    width = a_hbm.shape[0]
    sub = p_hbm.shape[0]
    slab = width // CHUNKS
    half_u, half_v = dinv_ref.shape[1], dinv_ref.shape[2]
    pole = lax.axis_index("pole")
    row = lax.axis_index("row")
    c = lax.axis_index("col")
    z = row // 2
    y = row % 2
    q = 2 * y + c
    mirror = z // 2

    def flip(v):
        return v + mirror * (GRID - 1 - 2 * v)

    zf, qf = flip(z), flip(q)

    def dev(zt, qt):
        return (pole, zt * 2 + qt // 2, qt % 2)

    def copy_to(src, dst, send, recv, where):
        return pltpu.make_async_remote_copy(
            src_ref=src, dst_ref=dst, send_sem=send, recv_sem=recv,
            device_id=where, device_id_type=MESH)

    def cols(k):
        return pl.ds(pl.multiple_of(k * width, width), width)

    def part(block, r):
        return pl.ds(pl.multiple_of(block * width + r * sub, sub), sub)

    loads = [
        pltpu.make_async_copy(pattern_hbm, pattern_ref, l_sem.at[0]),
        pltpu.make_async_copy(p_hbm.at[:, cols(z)], pbuf.at[part(q, z), :], l_sem.at[1]),
        pltpu.make_async_copy(a_hbm, a_ref, l_sem.at[2]),
        pltpu.make_async_copy(dinv_hbm, dinv_ref, l_sem.at[3]),
    ]
    for cp in loads:
        cp.start()

    barrier = pltpu.get_barrier_semaphore()
    me = z * GRID + q
    for d in range(1, GRID * GRID):
        other = (me + d) % (GRID * GRID)
        pl.semaphore_signal(barrier, inc=1, device_id=dev(other // GRID, other % GRID), device_id_type=MESH)
    pl.semaphore_wait(barrier, GRID * GRID - 1)

    core_mate = q + 1 - 2 * c
    across = q + 2 - 4 * y

    z_copies = []
    for d in (1, 3, 2):
        zt = (z + d) % GRID
        cp = copy_to(p_hbm.at[:, cols(zt)], pbuf.at[part(q, z), :], p_send.at[d], p_recv.at[q * GRID + z], dev(zt, q))
        cp.start()
        z_copies.append(cp)

    def a_copy(src, n, tz, tq, slot, chunk):
        rows = pl.ds(chunk * slab, slab)
        return copy_to(src.at[rows, :], abuf.at[flip(slot), rows, :], a_send.at[n * CHUNKS + chunk],
                       a_recv.at[flip(slot) * CHUNKS + chunk], dev(flip(tz), flip(tq)))

    def a_pass(step, src, chunk):
        for (cz, cq), routes in ROUTES.items():
            targets = numbered(routes)[step]
            if targets:
                @pl.when((zf == cz) & (qf == cq))
                def _():
                    for n, tz, tq, slot in targets:
                        a_copy(src, n, tz, tq, slot, chunk).start()

    for chunk in range(CHUNKS):
        a_pass(0, a_hbm, chunk)

    upper, odd = qf // 2, qf % 2
    away = 1 - zf
    slots = (
        flip((1 - upper) * away + upper * qf),
        flip((1 - upper) * 2 + upper * ((1 - odd) * 3 + odd * away)),
        flip((1 - upper) * 3 + upper * ((1 - odd) * away + odd * 2)),
    )

    def a_arrive(step):
        slot = slots[step]
        for chunk in range(CHUNKS):
            ref = abuf.at[slot, pl.ds(chunk * slab, slab), :]
            pltpu.make_async_copy(ref, ref, a_recv.at[slot * CHUNKS + chunk]).wait()
            a_pass(step + 1, abuf.at[slot], chunk)

    def p_wait(block, r):
        ref = pbuf.at[part(block, r), :]
        pltpu.make_async_copy(ref, ref, p_recv.at[block * GRID + r]).wait()

    layer_copies = []

    def p_share(src, r, d):
        for n, qt in ((0, across), (1, core_mate)):
            cp = copy_to(src, pbuf.at[part(q, r), :], f_send.at[2 * d + n], p_recv.at[q * GRID + r], dev(z, qt))
            cp.start()
            layer_copies.append(cp)

    p_share(p_hbm.at[:, cols(z)], z, 0)
    for cp in loads:
        cp.wait()
    for d in (1, 3, 2):
        r = (z + d) % GRID
        p_wait(q, r)
        p_share(pbuf.at[part(q, r), :], r, d)
    a_arrive(0)
    for d in (0, 1, 3, 2):
        r = (z + d) % GRID
        p_wait(across, r)
        ref = pbuf.at[part(across, r), :]
        cp = copy_to(ref, ref, g_send.at[d], p_recv.at[across * GRID + r], dev(z, core_mate))
        cp.start()
        layer_copies.append(cp)
    for block in (core_mate, core_mate + 2 - 4 * y):
        for r in range(GRID):
            p_wait(block, r)

    def lhat(block):
        rows = pl.ds(pl.multiple_of(block * width, width), width)
        return pbuf[rows, :] * pattern_ref[block, z].astype(jnp.float32)

    def dot_t(left, right):
        return lax.dot_general(left, right, (((0,), (0,)), ((), ())), precision=HIGHEST,
                               preferred_element_type=jnp.float32)

    acc[...] = dot_t(a_ref[...], lhat(z))
    for step in range(3):
        if step:
            a_arrive(step)
        slot = slots[step]
        slot_f = flip(slot)
        turned = (qf != zf) & (qf >= 2) & (slot_f < qf)

        @pl.when(turned)
        def _():
            acc[...] += dot_t(abuf[slot], lhat(slot))

        @pl.when(jnp.logical_not(turned))
        def _():
            acc[...] += jnp.dot(abuf[slot], lhat(slot), precision=HIGHEST, preferred_element_type=jnp.float32)

    product = acc[...]
    stage[...] = -(product * pattern_ref[q, z].astype(jnp.float32))
    out_copies = []
    for d in (1, 3, 2):
        zt = (z + d) % GRID
        cp = copy_to(stage.at[part(0, zt), :], off_ref.at[:, cols(z)], o_send.at[d], o_recv.at[z], dev(zt, q))
        cp.start()
        out_copies.append(cp)
    dpart[...] = dot_t(lhat(q), product)
    for d in (2, 1, 3):
        qt = (q + d) % GRID
        cp = copy_to(dpart.at[part(0, qt), :], dbuf.at[d - 1], d_send.at[d], d_recv.at[d - 1], dev(z, qt))
        cp.start()
        out_copies.append(cp)
    off_ref[:, cols(z)] = stage[part(0, z), :]
    total = dpart[part(0, q), :]
    for d in (1, 2, 3):
        pltpu.make_async_copy(dbuf.at[d - 1], dbuf.at[d - 1], d_recv.at[d - 1]).wait()
        total = total + dbuf[d - 1]
    for qt in range(GRID):
        yt, ct = qt // 2, qt % 2
        ebuf[qt] = total[yt * half_u:(yt + 1) * half_u, ct * half_v:(ct + 1) * half_v]
    e_copies = [copy_to(ebuf.at[qt], dfin.at[z], e_send.at[qt], e_recv.at[z], dev(q, qt)) for qt in range(GRID)]
    for qt in range(GRID):
        own = (q == z) & (q == qt)

        @pl.when(jnp.logical_not(own))
        def _():
            e_copies[qt].start()

        @pl.when(own)
        def _():
            dfin[z] = ebuf[qt]

    for d in (1, 3, 2):
        zs = (z + d) % GRID
        ref = off_ref.at[:, cols(zs)]
        pltpu.make_async_copy(ref, ref, o_recv.at[zs]).wait()
    for k in range(GRID):
        @pl.when(jnp.logical_not((q == z) & (z == k)))
        def _():
            pltpu.make_async_copy(dfin.at[k], dfin.at[k], e_recv.at[k]).wait()
        diag_ref[k] = dinv_ref[k] + dfin[k]

    for cp in z_copies + layer_copies + out_copies:
        cp.wait_send()
    for qt in range(GRID):
        @pl.when(jnp.logical_not((q == z) & (q == qt)))
        def _():
            e_copies[qt].wait_send()
    for (cz, cq), routes in ROUTES.items():
        @pl.when((zf == cz) & (qf == cq))
        def _():
            for targets in numbered(routes):
                for n, tz, tq, slot in targets:
                    for chunk in range(CHUNKS):
                        a_copy(a_ref, n, tz, tq, slot, chunk).wait_send()


def square_grid(inverse, panel, pattern, dinv):
    width = inverse.shape[3]
    sub, ncols = panel.shape[2], panel.shape[3]
    vmem = pl.BlockSpec(memory_space=pltpu.VMEM)
    dma = pltpu.SemaphoreType.DMA
    f32 = jnp.float32
    off, diagonal = pl.pallas_call(
        kernel,
        out_shape=(jax.ShapeDtypeStruct((sub, ncols), f32), jax.ShapeDtypeStruct(dinv.shape, f32)),
        in_specs=[pl.BlockSpec(memory_space=pl.ANY)] * 4,
        out_specs=(vmem, vmem),
        scratch_shapes=[
            pltpu.SMEM(pattern.shape, pattern.dtype),
            pltpu.VMEM((width, width), f32),
            pltpu.VMEM(dinv.shape, f32),
            dma((4,)),
            pltpu.VMEM((GRID, width, width), f32),
            pltpu.VMEM((GRID * width, width), f32),
            pltpu.VMEM((width, width), f32),
            pltpu.VMEM((width, width), f32),
            pltpu.VMEM((width, width), f32),
            pltpu.VMEM((GRID - 1, sub, width), f32),
            pltpu.VMEM((GRID,) + dinv.shape[1:], f32),
            pltpu.VMEM(dinv.shape, f32),
            dma((8 * CHUNKS,)), dma((GRID * CHUNKS,)), dma((GRID,)), dma((GRID * GRID,)), dma((2 * GRID,)), dma((GRID,)),
            dma((GRID,)), dma((GRID,)), dma((GRID,)), dma((GRID,)), dma((GRID,)), dma((GRID,)),
        ],
        compiler_params=pltpu.CompilerParams(
            collective_id=0, has_side_effects=True, vmem_limit_bytes=56 * 1024 * 1024),
    )(pattern, inverse.reshape(inverse.shape[2:]), panel.reshape(panel.shape[2:]), dinv)
    return off.reshape(panel.shape), diagonal


def fits_square_grid(mesh_shape, inverse, panel, pattern, dinv):
    n_row, n_col = mesh_shape["row"], mesh_shape["col"]
    width = inverse.shape[3]
    return (
        n_row == 2 * GRID and n_col == 2
        and inverse.shape[2] == width and width % 128 == 0
        and pattern.shape == (GRID, GRID)
        and panel.shape[2] * GRID == width and panel.shape[3] == GRID * width
        and dinv.shape == (GRID, width // n_row, width // n_col)
    )


def body(inverse, panel, pattern, dinv):
    sizes = {"row": lax.axis_size("row"), "col": lax.axis_size("col")}
    if fits_square_grid(sizes, inverse, panel, pattern, dinv):
        return square_grid(inverse, panel, pattern, dinv)
    return general_body(inverse, panel, pattern, dinv)


def solution(mesh):
    return jax.shard_map(
        body,
        mesh=mesh,
        in_specs=(
            P(("pole", "row"), "col", None, None),
            P(("pole", "row"), "col", None, None),
            P(),
            P("pole", "row", "col"),
        ),
        out_specs=(P(("pole", "row"), "col", None, None), P("pole", "row", "col")),
        check_vma=False,
    )
```

```python
import jax
import jax.numpy as jnp
from jax import lax
from jax.experimental import pallas as pl
from jax.experimental.pallas import tpu as pltpu
from jax.sharding import PartitionSpec as P


def swapped(value, axis, apart):
    mask = 2**apart
    pairs = [(source, source ^ mask) for source in range(lax.axis_size(axis))]
    return lax.ppermute(value, axis, pairs)


def group_flip(current, position, col_bits):
    if position < col_bits:
        return swapped(current, "col", position)
    return swapped(current, "row", position - col_bits)


def cross_flip(current, position, col_bits):
    if position < col_bits:
        return swapped(current, "col", position)
    return swapped(current, "row", position - col_bits)


def bit_at(device_at, position):
    return device_at >> position & 1


def collect(current, positions, device_at, col_bits):
    for position in positions:
        partner = group_flip(current, position, col_bits)
        upper_half = bit_at(device_at, position) == 1
        current = jnp.where(
            upper_half,
            jnp.concatenate([partner, current], 0),
            jnp.concatenate([current, partner], 0),
        )
    return current


def reduce_split(current, positions, device_at, col_bits):
    for position in positions:
        halfway = current.shape[0] // 2
        mine_bit = bit_at(device_at, position)
        kept_half = lax.dynamic_slice_in_dim(current, mine_bit * halfway, halfway, 0)
        sent_half = lax.dynamic_slice_in_dim(current, (1 - mine_bit) * halfway, halfway, 0)
        current = kept_half + group_flip(sent_half, position, col_bits)
    return current


def relabel(current, targets, device_at, col_bits):
    mapping = list(range(len(targets)))
    for column in range(len(targets)):
        if mapping[column] != targets[column]:
            lead_bit = mapping[column]
            other_bit = targets[column]
            shifted = cross_flip(cross_flip(current, lead_bit, col_bits), other_bit, col_bits)
            unequal = bit_at(device_at, lead_bit) != bit_at(device_at, other_bit)
            current = jnp.where(unequal, shifted, current)
            mapping = [
                other_bit if element == lead_bit else lead_bit if element == other_bit else element
                for element in mapping
            ]
    return current


def general_body(inverse, panel, pattern, dinv):
    n_row = lax.axis_size("row")
    n_col = lax.axis_size("col")
    device_at = lax.axis_index("row") * n_col + lax.axis_index("col")
    grid_rows = min(8, n_row // 2)
    grid_cols = n_row * n_col // grid_rows
    col_bits = n_col.bit_length() - 1
    total_bits = (n_row * n_col).bit_length() - 1
    high_bits = grid_rows.bit_length() - 1
    side_bits = total_bits - high_bits
    grid_row = device_at // grid_cols
    grid_col = device_at % grid_cols
    rows_dev, col_count = (panel.shape[2], panel.shape[3])
    nblocks, sup_count = pattern.shape
    sup_width = col_count // sup_count
    first_row = (grid_col * grid_rows + grid_row) * rows_dev
    global_rows = first_row + jnp.arange(rows_dev, dtype=jnp.int32)
    onehot = (
        global_rows[:, None] // sup_width == jnp.arange(nblocks, dtype=jnp.int32)[None, :]
    ).astype(jnp.float32)
    keep_sup = jnp.dot(onehot, pattern.astype(jnp.float32), precision=lax.Precision.HIGHEST)
    keep_piece = jnp.broadcast_to(keep_sup[:, :, None], (rows_dev, sup_count, sup_width)).reshape(
        rows_dev, col_count
    )
    lhat_piece = panel.reshape(rows_dev, col_count) * keep_piece
    inverse_block = inverse.reshape(inverse.shape[2], inverse.shape[3])
    gathered = collect(lhat_piece, list(range(side_bits, total_bits)), device_at, col_bits)
    partial_sum = jnp.dot(
        inverse_block, gathered, precision=lax.Precision.HIGHEST, preferred_element_type=jnp.float32
    )
    row_piece = reduce_split(partial_sum, list(range(side_bits - 1, -1, -1)), device_at, col_bits)
    backward = [(bit_slot + side_bits) % total_bits for bit_slot in range(total_bits)]
    product_piece = relabel(row_piece, backward, device_at, col_bits)
    diag_terms = jnp.einsum(
        "rkw,rkv->kwv",
        lhat_piece.reshape(rows_dev, sup_count, sup_width),
        product_piece.reshape(rows_dev, sup_count, sup_width),
        precision=lax.Precision.HIGHEST,
    )
    arranged = diag_terms.reshape(sup_count, n_row, sup_width // n_row, n_col, sup_width // n_col)
    arranged = arranged.transpose(1, 3, 0, 2, 4).reshape(
        n_row * n_col, sup_count, sup_width // n_row, sup_width // n_col
    )
    diagonal = dinv + lax.psum_scatter(arranged, ("row", "col"), scatter_dimension=0, tiled=True)[0]
    off_diagonal = (-(product_piece * keep_piece)).reshape(panel.shape)
    return (off_diagonal, diagonal)


MESH = pl.DeviceIdType.MESH
HIGHEST = lax.Precision.HIGHEST
GRID = 4
CHUNKS = 4

ROUTES = {
    (0, 0): ([(1, 0, 0)], [], [(1, 0, 2)], [(1, 0, 3)]),
    (0, 1): ([(0, 0, 1)], [], [(0, 2, 1)], [(0, 3, 1)]),
    (0, 2): ([(0, 0, 2)], [], [(0, 3, 2)], []),
    (0, 3): ([(0, 0, 3)], [], [], []),
    (1, 0): ([(1, 1, 0)], [(2, 0, 0)], [(1, 2, 0)], [(1, 3, 0)]),
    (1, 1): ([(0, 1, 1), (2, 1, 1)], [(2, 1, 0)], [(0, 1, 2)], [(0, 1, 3)]),
    (1, 2): ([(1, 1, 2)], [(0, 2, 2)], [(0, 2, 3), (1, 3, 2)], []),
    (1, 3): ([(1, 1, 3)], [(0, 3, 3)], [], []),
}

RELAY_AT = (
    {(1, 0): (0,), (1, 1): (0,), (1, 2): (0,)},
    {(0, 0): (1,), (1, 1): (1,)},
    {(0, 0): (2,), (1, 1): (2,), (1, 2): (1,), (1, 3): (0,)},
    {(0, 2): (1,)},
    {(1, 0): (1,), (0, 1): (1,)},
    {(1, 0): (2,), (0, 1): (2,)},
)


def numbered(routes):
    count = 0
    out = []
    for targets in routes:
        out.append([(count + n,) + t for n, t in enumerate(targets)])
        count += len(targets)
    return out


def kernel(pattern_hbm, a_hbm, p_hbm, dinv_hbm, off_ref, diag_ref,
           pattern_ref, a_ref, dinv_ref, l_sem, abuf, pbuf, acc, stage, dpart, dbuf, ebuf, dfin,
           a_send, a_recv, p_send, p_recv, f_send, g_send, o_send, o_recv,
           d_send, d_recv, e_send, e_recv):
    width = a_hbm.shape[0]
    sub = p_hbm.shape[0]
    slab = width // CHUNKS
    half_u, half_v = dinv_ref.shape[1], dinv_ref.shape[2]
    pole = lax.axis_index("pole")
    row = lax.axis_index("row")
    c = lax.axis_index("col")
    z = row // 2
    y = row % 2
    q = 2 * y + c
    mirror = z // 2

    def flip(v):
        return v + mirror * (GRID - 1 - 2 * v)

    zf, qf = flip(z), flip(q)

    def dev(zt, qt):
        return (pole, zt * 2 + qt // 2, qt % 2)

    def copy_to(src, dst, send, recv, where):
        return pltpu.make_async_remote_copy(
            src_ref=src, dst_ref=dst, send_sem=send, recv_sem=recv,
            device_id=where, device_id_type=MESH)

    def cols(k):
        return pl.ds(pl.multiple_of(k * width, width), width)

    def part(block, r):
        return pl.ds(pl.multiple_of(block * width + r * sub, sub), sub)

    loads = [
        pltpu.make_async_copy(pattern_hbm, pattern_ref, l_sem.at[0]),
        pltpu.make_async_copy(p_hbm.at[:, cols(z)], pbuf.at[part(q, z), :], l_sem.at[1]),
        pltpu.make_async_copy(a_hbm, a_ref, l_sem.at[2]),
        pltpu.make_async_copy(dinv_hbm, dinv_ref, l_sem.at[3]),
    ]
    for cp in loads:
        cp.start()

    barrier = pltpu.get_barrier_semaphore()
    for d in range(1, GRID):
        pl.semaphore_signal(barrier, inc=1, device_id=dev(z, (q + d) % GRID), device_id_type=MESH)
        pl.semaphore_signal(barrier, inc=1, device_id=dev((z + d) % GRID, q), device_id_type=MESH)
    pl.semaphore_wait(barrier, 2 * (GRID - 1))

    core_mate = q + 1 - 2 * c
    across = q + 2 - 4 * y

    def a_copy(src, n, tz, tq, slot, chunk):
        rows = pl.ds(chunk * slab, slab)
        return copy_to(src.at[rows, :], abuf.at[flip(slot), rows, :], a_send.at[n * CHUNKS + chunk],
                       a_recv.at[flip(slot) * CHUNKS + chunk], dev(flip(tz), flip(tq)))

    for (cz, cq), routes in ROUTES.items():
        @pl.when((zf == cz) & (qf == cq))
        def _():
            for chunk in range(CHUNKS):
                for n, tz, tq, slot in numbered(routes)[0]:
                    a_copy(a_hbm, n, tz, tq, slot, chunk).start()

    z_copies = []
    for d in (1, 3, 2):
        zt = (z + d) % GRID
        cp = copy_to(p_hbm.at[:, cols(zt)], pbuf.at[part(q, z), :], p_send.at[d], p_recv.at[q * GRID + z], dev(zt, q))
        cp.start()
        z_copies.append(cp)

    upper, odd = qf // 2, qf % 2
    away = 1 - zf
    slots = (
        flip((1 - upper) * away + upper * qf),
        flip((1 - upper) * 2 + upper * ((1 - odd) * 3 + odd * away)),
        flip((1 - upper) * 3 + upper * ((1 - odd) * away + odd * 2)),
    )

    def a_wait(step, chunk):
        slot = slots[step]
        ref = abuf.at[slot, pl.ds(chunk * slab, slab), :]
        pltpu.make_async_copy(ref, ref, a_recv.at[slot * CHUNKS + chunk]).wait()

    def a_relay(place):
        for (cz, cq), routes in ROUTES.items():
            steps = RELAY_AT[place].get((cz, cq), ())
            if steps:
                @pl.when((zf == cz) & (qf == cq))
                def _():
                    for step in steps:
                        for chunk in range(CHUNKS):
                            a_wait(step, chunk)
                            for n, tz, tq, slot in numbered(routes)[step + 1]:
                                a_copy(abuf.at[slots[step]], n, tz, tq, slot, chunk).start()

    def a_arrive(step):
        for (cz, cq), routes in ROUTES.items():
            if not routes[step + 1]:
                @pl.when((zf == cz) & (qf == cq))
                def _():
                    for chunk in range(CHUNKS):
                        a_wait(step, chunk)

    def p_wait(block, r):
        ref = pbuf.at[part(block, r), :]
        pltpu.make_async_copy(ref, ref, p_recv.at[block * GRID + r]).wait()

    layer_copies = []

    def p_share(src, r, d):
        for n, qt in ((0, across), (1, core_mate)):
            cp = copy_to(src, pbuf.at[part(q, r), :], f_send.at[2 * d + n], p_recv.at[q * GRID + r], dev(z, qt))
            cp.start()
            layer_copies.append(cp)

    p_share(p_hbm.at[:, cols(z)], z, 0)
    for cp in loads:
        cp.wait()
    a_relay(0)
    for place, d in enumerate((1, 3, 2)):
        r = (z + d) % GRID
        p_wait(q, r)
        p_share(pbuf.at[part(q, r), :], r, d)
        a_relay(place + 1)
    a_relay(4)
    for d in (0, 1, 3, 2):
        r = (z + d) % GRID
        p_wait(across, r)
        ref = pbuf.at[part(across, r), :]
        cp = copy_to(ref, ref, g_send.at[d], p_recv.at[across * GRID + r], dev(z, core_mate))
        cp.start()
        layer_copies.append(cp)
    a_relay(5)
    for block in (core_mate, core_mate + 2 - 4 * y):
        for r in range(GRID):
            p_wait(block, r)

    def lhat(block):
        rows = pl.ds(pl.multiple_of(block * width, width), width)
        return pbuf[rows, :] * pattern_ref[block, z].astype(jnp.float32)

    def dot_t(left, right):
        return lax.dot_general(left, right, (((0,), (0,)), ((), ())), precision=HIGHEST,
                               preferred_element_type=jnp.float32)

    acc[...] = dot_t(a_ref[...], lhat(z))
    for step in range(3):
        a_arrive(step)
        slot = slots[step]
        slot_f = flip(slot)
        turned = (qf != zf) & (qf >= 2) & (slot_f < qf)

        @pl.when(turned)
        def _():
            acc[...] += dot_t(abuf[slot], lhat(slot))

        @pl.when(jnp.logical_not(turned))
        def _():
            acc[...] += jnp.dot(abuf[slot], lhat(slot), precision=HIGHEST, preferred_element_type=jnp.float32)

    product = acc[...]
    stage[...] = -(product * pattern_ref[q, z].astype(jnp.float32))
    out_copies = []
    for d in (1, 3, 2):
        zt = (z + d) % GRID
        cp = copy_to(stage.at[part(0, zt), :], off_ref.at[:, cols(z)], o_send.at[d], o_recv.at[z], dev(zt, q))
        cp.start()
        out_copies.append(cp)
    terms = dot_t(lhat(q), product)
    for zt in range(GRID):
        for qt in range(GRID):
            u, v = zt * sub + (qt // 2) * half_u, (qt % 2) * half_v
            dpart[qt, zt] = terms[u:u + half_u, v:v + half_v]
    for d in (2, 1, 3):
        qt = (q + d) % GRID
        cp = copy_to(dpart.at[qt], dbuf.at[d - 1], d_send.at[d], d_recv.at[d - 1], dev(z, qt))
        cp.start()
        out_copies.append(cp)
    off_ref[:, cols(z)] = stage[part(0, z), :]
    total = dpart[q]
    for d in (1, 2, 3):
        pltpu.make_async_copy(dbuf.at[d - 1], dbuf.at[d - 1], d_recv.at[d - 1]).wait()
        total = total + dbuf[d - 1]
    ebuf[...] = total
    for d in (1, 3, 2):
        zt = (z + d) % GRID
        cp = copy_to(ebuf.at[zt], dfin.at[z], e_send.at[d], e_recv.at[z], dev(zt, q))
        cp.start()
        out_copies.append(cp)
    diag_ref[z] = dinv_ref[z] + ebuf[z]
    for d in (1, 3, 2):
        k = (z + d) % GRID
        pltpu.make_async_copy(dfin.at[k], dfin.at[k], e_recv.at[k]).wait()
        diag_ref[k] = dinv_ref[k] + dfin[k]
    for d in (1, 3, 2):
        zs = (z + d) % GRID
        ref = off_ref.at[:, cols(zs)]
        pltpu.make_async_copy(ref, ref, o_recv.at[zs]).wait()
    for cp in z_copies + layer_copies + out_copies:
        cp.wait_send()
    for (cz, cq), routes in ROUTES.items():
        @pl.when((zf == cz) & (qf == cq))
        def _():
            for targets in numbered(routes):
                for n, tz, tq, slot in targets:
                    for chunk in range(CHUNKS):
                        a_copy(a_ref, n, tz, tq, slot, chunk).wait_send()


def square_grid(inverse, panel, pattern, dinv):
    width = inverse.shape[3]
    sub, ncols = panel.shape[2], panel.shape[3]
    vmem = pl.BlockSpec(memory_space=pltpu.VMEM)
    dma = pltpu.SemaphoreType.DMA
    f32 = jnp.float32
    off, diagonal = pl.pallas_call(
        kernel,
        out_shape=(jax.ShapeDtypeStruct((sub, ncols), f32), jax.ShapeDtypeStruct(dinv.shape, f32)),
        in_specs=[pl.BlockSpec(memory_space=pltpu.HBM)] * 4,
        out_specs=(vmem, vmem),
        scratch_shapes=[
            pltpu.SMEM(pattern.shape, pattern.dtype),
            pltpu.VMEM((width, width), f32),
            pltpu.VMEM(dinv.shape, f32),
            dma((4,)),
            pltpu.VMEM((GRID, width, width), f32),
            pltpu.VMEM((GRID * width, width), f32),
            pltpu.VMEM((width, width), f32),
            pltpu.VMEM((width, width), f32),
            pltpu.VMEM((GRID,) + dinv.shape, f32),
            pltpu.VMEM((GRID - 1,) + dinv.shape, f32),
            pltpu.VMEM(dinv.shape, f32),
            pltpu.VMEM(dinv.shape, f32),
            dma((8 * CHUNKS,)), dma((GRID * CHUNKS,)), dma((GRID,)), dma((GRID * GRID,)), dma((2 * GRID,)), dma((GRID,)),
            dma((GRID,)), dma((GRID,)), dma((GRID,)), dma((GRID,)), dma((GRID,)), dma((GRID,)),
        ],
        compiler_params=pltpu.CompilerParams(
            collective_id=0, has_side_effects=True, vmem_limit_bytes=56 * 1024 * 1024),
    )(pattern, inverse.reshape(inverse.shape[2:]), panel.reshape(panel.shape[2:]), dinv)
    return off.reshape(panel.shape), diagonal


def fits_square_grid(mesh_shape, inverse, panel, pattern, dinv):
    n_row, n_col = mesh_shape["row"], mesh_shape["col"]
    width = inverse.shape[3]
    return (
        n_row == 2 * GRID and n_col == 2
        and inverse.shape[2] == width and width % 128 == 0
        and pattern.shape == (GRID, GRID)
        and panel.shape[2] * GRID == width and panel.shape[3] == GRID * width
        and dinv.shape == (GRID, width // n_row, width // n_col)
    )


def body(inverse, panel, pattern, dinv):
    sizes = {"row": lax.axis_size("row"), "col": lax.axis_size("col")}
    if fits_square_grid(sizes, inverse, panel, pattern, dinv):
        return square_grid(inverse, panel, pattern, dinv)
    return general_body(inverse, panel, pattern, dinv)


def solution(mesh):
    return jax.shard_map(
        body,
        mesh=mesh,
        in_specs=(
            P(("pole", "row"), "col", None, None),
            P(("pole", "row"), "col", None, None),
            P(),
            P("pole", "row", "col"),
        ),
        out_specs=(P(("pole", "row"), "col", None, None), P("pole", "row", "col")),
        check_vma=False,
    )
```

```python
import jax
import jax.numpy as jnp
from jax import lax
from jax.experimental import pallas as pl
from jax.experimental.pallas import tpu as pltpu
from jax.sharding import PartitionSpec as P


def swapped(value, axis, apart):
    mask = 2**apart
    pairs = [(source, source ^ mask) for source in range(lax.axis_size(axis))]
    return lax.ppermute(value, axis, pairs)


def group_flip(current, position, col_bits):
    if position < col_bits:
        return swapped(current, "col", position)
    return swapped(current, "row", position - col_bits)


def cross_flip(current, position, col_bits):
    if position < col_bits:
        return swapped(current, "col", position)
    return swapped(current, "row", position - col_bits)


def bit_at(device_at, position):
    return device_at >> position & 1


def collect(current, positions, device_at, col_bits):
    for position in positions:
        partner = group_flip(current, position, col_bits)
        upper_half = bit_at(device_at, position) == 1
        current = jnp.where(
            upper_half,
            jnp.concatenate([partner, current], 0),
            jnp.concatenate([current, partner], 0),
        )
    return current


def reduce_split(current, positions, device_at, col_bits):
    for position in positions:
        halfway = current.shape[0] // 2
        mine_bit = bit_at(device_at, position)
        kept_half = lax.dynamic_slice_in_dim(current, mine_bit * halfway, halfway, 0)
        sent_half = lax.dynamic_slice_in_dim(current, (1 - mine_bit) * halfway, halfway, 0)
        current = kept_half + group_flip(sent_half, position, col_bits)
    return current


def relabel(current, targets, device_at, col_bits):
    mapping = list(range(len(targets)))
    for column in range(len(targets)):
        if mapping[column] != targets[column]:
            lead_bit = mapping[column]
            other_bit = targets[column]
            shifted = cross_flip(cross_flip(current, lead_bit, col_bits), other_bit, col_bits)
            unequal = bit_at(device_at, lead_bit) != bit_at(device_at, other_bit)
            current = jnp.where(unequal, shifted, current)
            mapping = [
                other_bit if element == lead_bit else lead_bit if element == other_bit else element
                for element in mapping
            ]
    return current


def general_body(inverse, panel, pattern, dinv):
    n_row = lax.axis_size("row")
    n_col = lax.axis_size("col")
    device_at = lax.axis_index("row") * n_col + lax.axis_index("col")
    grid_rows = min(8, n_row // 2)
    grid_cols = n_row * n_col // grid_rows
    col_bits = n_col.bit_length() - 1
    total_bits = (n_row * n_col).bit_length() - 1
    high_bits = grid_rows.bit_length() - 1
    side_bits = total_bits - high_bits
    grid_row = device_at // grid_cols
    grid_col = device_at % grid_cols
    rows_dev, col_count = (panel.shape[2], panel.shape[3])
    nblocks, sup_count = pattern.shape
    sup_width = col_count // sup_count
    first_row = (grid_col * grid_rows + grid_row) * rows_dev
    global_rows = first_row + jnp.arange(rows_dev, dtype=jnp.int32)
    onehot = (
        global_rows[:, None] // sup_width == jnp.arange(nblocks, dtype=jnp.int32)[None, :]
    ).astype(jnp.float32)
    keep_sup = jnp.dot(onehot, pattern.astype(jnp.float32), precision=lax.Precision.HIGHEST)
    keep_piece = jnp.broadcast_to(keep_sup[:, :, None], (rows_dev, sup_count, sup_width)).reshape(
        rows_dev, col_count
    )
    lhat_piece = panel.reshape(rows_dev, col_count) * keep_piece
    inverse_block = inverse.reshape(inverse.shape[2], inverse.shape[3])
    gathered = collect(lhat_piece, list(range(side_bits, total_bits)), device_at, col_bits)
    partial_sum = jnp.dot(
        inverse_block, gathered, precision=lax.Precision.HIGHEST, preferred_element_type=jnp.float32
    )
    row_piece = reduce_split(partial_sum, list(range(side_bits - 1, -1, -1)), device_at, col_bits)
    backward = [(bit_slot + side_bits) % total_bits for bit_slot in range(total_bits)]
    product_piece = relabel(row_piece, backward, device_at, col_bits)
    diag_terms = jnp.einsum(
        "rkw,rkv->kwv",
        lhat_piece.reshape(rows_dev, sup_count, sup_width),
        product_piece.reshape(rows_dev, sup_count, sup_width),
        precision=lax.Precision.HIGHEST,
    )
    arranged = diag_terms.reshape(sup_count, n_row, sup_width // n_row, n_col, sup_width // n_col)
    arranged = arranged.transpose(1, 3, 0, 2, 4).reshape(
        n_row * n_col, sup_count, sup_width // n_row, sup_width // n_col
    )
    diagonal = dinv + lax.psum_scatter(arranged, ("row", "col"), scatter_dimension=0, tiled=True)[0]
    off_diagonal = (-(product_piece * keep_piece)).reshape(panel.shape)
    return (off_diagonal, diagonal)


MESH = pl.DeviceIdType.MESH
HIGHEST = lax.Precision.HIGHEST
GRID = 4
CHUNKS = 4
PIECES = 2

ROUTES = {
    (0, 0): ([(1, 0, 0)], [], [(1, 0, 2)], [(1, 0, 3)]),
    (0, 1): ([(0, 0, 1)], [], [(0, 2, 1)], [(0, 3, 1)]),
    (0, 2): ([(0, 0, 2)], [], [(0, 3, 2)], []),
    (0, 3): ([(0, 0, 3)], [], [], []),
    (1, 0): ([(1, 1, 0)], [(2, 0, 0)], [(1, 2, 0)], [(1, 3, 0)]),
    (1, 1): ([(0, 1, 1), (2, 1, 1)], [(2, 1, 0)], [(0, 1, 2)], [(0, 1, 3)]),
    (1, 2): ([(1, 1, 2)], [(0, 2, 2)], [(0, 2, 3), (1, 3, 2)], []),
    (1, 3): ([(1, 1, 3)], [(0, 3, 3)], [], []),
}

def one(step):
    return [(step, chunk) for chunk in range(CHUNKS)]


def both(chunks):
    return [(step, chunk) for chunk in chunks for step in (1, 2)]


RELAY_AT = (
    {(1, 0): one(0), (1, 1): one(0) + both(range(CHUNKS)), (1, 2): one(0), (0, 0): both(range(CHUNKS))},
    {},
    {(1, 2): one(1), (1, 3): one(0)},
    {(0, 2): one(1)},
    {(1, 0): both((0,)), (0, 1): both((0,))},
    {(1, 0): both((1,)), (0, 1): both((1,))},
    {(1, 0): both((2,)), (0, 1): both((2,))},
    {(1, 0): both((3,)), (0, 1): both((3,))},
)


def numbered(routes):
    count = 0
    out = []
    for targets in routes:
        out.append([(count + n,) + t for n, t in enumerate(targets)])
        count += len(targets)
    return out


def kernel(pattern_hbm, a_hbm, p_hbm, dinv_hbm, off_ref, diag_ref,
           pattern_ref, a_ref, dinv_ref, l_sem, w_sem, abuf, pbuf, acc, stage, dpart, dbuf, ebuf, dfin,
           a_send, a_recv, p_send, p_recv, f_send, g_send, o_send, o_recv,
           d_send, d_recv, e_send, e_recv):
    width = a_hbm.shape[0]
    sub = p_hbm.shape[0]
    slab = width // CHUNKS
    half_u, half_v = dinv_ref.shape[1], dinv_ref.shape[2]
    pole = lax.axis_index("pole")
    row = lax.axis_index("row")
    c = lax.axis_index("col")
    z = row // 2
    y = row % 2
    q = 2 * y + c
    mirror = z // 2

    def flip(v):
        return v + mirror * (GRID - 1 - 2 * v)

    zf, qf = flip(z), flip(q)

    def dev(zt, qt):
        return (pole, zt * 2 + qt // 2, qt % 2)

    def copy_to(src, dst, send, recv, where):
        return pltpu.make_async_remote_copy(
            src_ref=src, dst_ref=dst, send_sem=send, recv_sem=recv,
            device_id=where, device_id_type=MESH)

    def cols(k):
        return pl.ds(pl.multiple_of(k * width, width), width)

    def part(block, r):
        return pl.ds(pl.multiple_of(block * width + r * sub, sub), sub)

    loads = [
        pltpu.make_async_copy(pattern_hbm, pattern_ref, l_sem.at[0]),
        pltpu.make_async_copy(p_hbm.at[:, cols(z)], pbuf.at[part(q, z), :], l_sem.at[1]),
        pltpu.make_async_copy(a_hbm, a_ref, l_sem.at[2]),
        pltpu.make_async_copy(dinv_hbm, dinv_ref, l_sem.at[3]),
    ]
    for cp in loads:
        cp.start()

    barrier = pltpu.get_barrier_semaphore()
    for d in range(1, GRID):
        pl.semaphore_signal(barrier, inc=1, device_id=dev(z, (q + d) % GRID), device_id_type=MESH)
        pl.semaphore_signal(barrier, inc=1, device_id=dev((z + d) % GRID, q), device_id_type=MESH)
    pl.semaphore_wait(barrier, 2 * (GRID - 1))

    core_mate = q + 1 - 2 * c
    across = q + 2 - 4 * y

    def a_copy(src, n, tz, tq, slot, chunk):
        rows = pl.ds(chunk * slab, slab)
        return copy_to(src.at[rows, :], abuf.at[flip(slot), rows, :], a_send.at[n * CHUNKS + chunk],
                       a_recv.at[flip(slot) * CHUNKS + chunk], dev(flip(tz), flip(tq)))

    for (cz, cq), routes in ROUTES.items():
        @pl.when((zf == cz) & (qf == cq))
        def _():
            for chunk in range(CHUNKS):
                for n, tz, tq, slot in numbered(routes)[0]:
                    a_copy(a_hbm, n, tz, tq, slot, chunk).start()

    z_copies = []
    for d in (1, 3, 2):
        zt = (z + d) % GRID
        cp = copy_to(p_hbm.at[:, cols(zt)], pbuf.at[part(q, z), :], p_send.at[d], p_recv.at[q * GRID + z], dev(zt, q))
        cp.start()
        z_copies.append(cp)

    upper, odd = qf // 2, qf % 2
    away = 1 - zf
    slots = (
        flip((1 - upper) * away + upper * qf),
        flip((1 - upper) * 2 + upper * ((1 - odd) * 3 + odd * away)),
        flip((1 - upper) * 3 + upper * ((1 - odd) * away + odd * 2)),
    )

    def a_wait(step, chunk):
        slot = slots[step]
        ref = abuf.at[slot, pl.ds(chunk * slab, slab), :]
        pltpu.make_async_copy(ref, ref, a_recv.at[slot * CHUNKS + chunk]).wait()

    def a_relay(place):
        for (cz, cq), routes in ROUTES.items():
            steps = RELAY_AT[place].get((cz, cq), ())
            if steps:
                @pl.when((zf == cz) & (qf == cq))
                def _():
                    for step, chunk in steps:
                        a_wait(step, chunk)
                        for n, tz, tq, slot in numbered(routes)[step + 1]:
                            a_copy(abuf.at[slots[step]], n, tz, tq, slot, chunk).start()

    def a_arrive(step):
        for (cz, cq), routes in ROUTES.items():
            if not routes[step + 1]:
                @pl.when((zf == cz) & (qf == cq))
                def _():
                    for chunk in range(CHUNKS):
                        a_wait(step, chunk)

    def p_wait(block, r):
        ref = pbuf.at[part(block, r), :]
        pltpu.make_async_copy(ref, ref, p_recv.at[block * GRID + r]).wait()

    layer_copies = []

    def p_share(src, r, d):
        for n, qt in ((0, across), (1, core_mate)):
            cp = copy_to(src, pbuf.at[part(q, r), :], f_send.at[2 * d + n], p_recv.at[q * GRID + r], dev(z, qt))
            cp.start()
            layer_copies.append(cp)

    p_share(p_hbm.at[:, cols(z)], z, 0)
    for cp in loads:
        cp.wait()
    a_relay(0)
    for place, d in enumerate((1, 3, 2)):
        r = (z + d) % GRID
        p_wait(q, r)
        p_share(pbuf.at[part(q, r), :], r, d)
        a_relay(place + 1)
    for place, d in enumerate((0, 1, 3, 2)):
        a_relay(4 + place)
        r = (z + d) % GRID
        p_wait(across, r)
        ref = pbuf.at[part(across, r), :]
        cp = copy_to(ref, ref, g_send.at[d], p_recv.at[across * GRID + r], dev(z, core_mate))
        cp.start()
        layer_copies.append(cp)
    for block in (core_mate, core_mate + 2 - 4 * y):
        for r in range(GRID):
            p_wait(block, r)

    def lhat(block):
        rows = pl.ds(pl.multiple_of(block * width, width), width)
        return pbuf[rows, :] * pattern_ref[block, z].astype(jnp.float32)

    def dot_t(left, right):
        return lax.dot_general(left, right, (((0,), (0,)), ((), ())), precision=HIGHEST,
                               preferred_element_type=jnp.float32)

    acc[...] = dot_t(a_ref[...], lhat(z))
    for step in range(3):
        a_arrive(step)
        slot = slots[step]
        slot_f = flip(slot)
        turned = (qf != zf) & (qf >= 2) & (slot_f < qf)

        @pl.when(turned)
        def _():
            acc[...] += dot_t(abuf[slot], lhat(slot))

        @pl.when(jnp.logical_not(turned))
        def _():
            acc[...] += jnp.dot(abuf[slot], lhat(slot), precision=HIGHEST, preferred_element_type=jnp.float32)

    product = acc[...]
    stage[...] = -(product * pattern_ref[q, z].astype(jnp.float32))
    out_copies = []
    for d in (1, 3, 2):
        zt = (z + d) % GRID
        cp = copy_to(stage.at[part(0, zt), :], off_ref.at[:, cols(z)], o_send.at[d], o_recv.at[z], dev(zt, q))
        cp.start()
        out_copies.append(cp)
    terms = dot_t(lhat(q), product)
    for zt in range(GRID):
        for qt in range(GRID):
            u, v = zt * sub + (qt // 2) * half_u, (qt % 2) * half_v
            dpart[qt, zt] = terms[u:u + half_u, v:v + half_v]
    for d in (2, 1, 3):
        qt = (q + d) % GRID
        cp = copy_to(dpart.at[qt], dbuf.at[d - 1], d_send.at[d], d_recv.at[d - 1], dev(z, qt))
        cp.start()
        out_copies.append(cp)
    writes = [pltpu.make_async_copy(stage.at[part(0, z), :], off_ref.at[:, cols(z)], w_sem.at[0])]
    writes[0].start()
    total = dpart[q]
    for d in (1, 2, 3):
        pltpu.make_async_copy(dbuf.at[d - 1], dbuf.at[d - 1], d_recv.at[d - 1]).wait()
        total = total + dbuf[d - 1]
    ebuf[...] = total
    for d in (1, 3, 2):
        zt = (z + d) % GRID
        cp = copy_to(ebuf.at[zt], dfin.at[z], e_send.at[d], e_recv.at[z], dev(zt, q))
        cp.start()
        out_copies.append(cp)
    dinv_ref[z] = dinv_ref[z] + ebuf[z]
    for d in (1, 3, 2):
        k = (z + d) % GRID
        pltpu.make_async_copy(dfin.at[k], dfin.at[k], e_recv.at[k]).wait()
        dinv_ref[k] = dinv_ref[k] + dfin[k]
    writes.append(pltpu.make_async_copy(dinv_ref, diag_ref, w_sem.at[1]))
    writes[1].start()
    for d in (1, 3, 2):
        zs = (z + d) % GRID
        ref = off_ref.at[:, cols(zs)]
        pltpu.make_async_copy(ref, ref, o_recv.at[zs]).wait()
    for cp in writes:
        cp.wait()
    for cp in z_copies + layer_copies + out_copies:
        cp.wait_send()
    for (cz, cq), routes in ROUTES.items():
        @pl.when((zf == cz) & (qf == cq))
        def _():
            for targets in numbered(routes):
                for n, tz, tq, slot in targets:
                    for chunk in range(CHUNKS):
                        a_copy(a_ref, n, tz, tq, slot, chunk).wait_send()


def hand_over(off_in, diag_in, off_out, diag_out, off_held, diag_held, off_sem, diag_sem):
    rows = off_in.shape[0] // PIECES
    pairs = [(
        pltpu.make_async_copy(diag_in, diag_held, diag_sem.at[0]),
        pltpu.make_async_copy(diag_held, diag_out, diag_sem.at[1]),
    )]
    for n in range(PIECES):
        piece = pl.ds(n * rows, rows)
        pairs.append((
            pltpu.make_async_copy(off_in.at[piece, :], off_held.at[piece, :], off_sem.at[0, n]),
            pltpu.make_async_copy(off_held.at[piece, :], off_out.at[piece, :], off_sem.at[1, n]),
        ))
    for load, store in pairs:
        load.start()
    for load, store in pairs:
        load.wait()
        store.start()
    for load, store in pairs:
        store.wait()


def square_grid(inverse, panel, pattern, dinv):
    width = inverse.shape[3]
    sub, ncols = panel.shape[2], panel.shape[3]
    hbm = pl.BlockSpec(memory_space=pltpu.HBM)
    dma = pltpu.SemaphoreType.DMA
    f32 = jnp.float32
    off, diagonal = pl.pallas_call(
        kernel,
        out_shape=(jax.ShapeDtypeStruct((sub, ncols), f32), jax.ShapeDtypeStruct(dinv.shape, f32)),
        in_specs=[hbm] * 4,
        out_specs=(hbm, hbm),
        scratch_shapes=[
            pltpu.SMEM(pattern.shape, pattern.dtype),
            pltpu.VMEM((width, width), f32),
            pltpu.VMEM(dinv.shape, f32),
            dma((4,)),
            dma((2,)),
            pltpu.VMEM((GRID, width, width), f32),
            pltpu.VMEM((GRID * width, width), f32),
            pltpu.VMEM((width, width), f32),
            pltpu.VMEM((width, width), f32),
            pltpu.VMEM((GRID,) + dinv.shape, f32),
            pltpu.VMEM((GRID - 1,) + dinv.shape, f32),
            pltpu.VMEM(dinv.shape, f32),
            pltpu.VMEM(dinv.shape, f32),
            dma((8 * CHUNKS,)), dma((GRID * CHUNKS,)), dma((GRID,)), dma((GRID * GRID,)), dma((2 * GRID,)), dma((GRID,)),
            dma((GRID,)), dma((GRID,)), dma((GRID,)), dma((GRID,)), dma((GRID,)), dma((GRID,)),
        ],
        compiler_params=pltpu.CompilerParams(
            collective_id=0, has_side_effects=True, vmem_limit_bytes=56 * 1024 * 1024),
    )(pattern, inverse.reshape(inverse.shape[2:]), panel.reshape(panel.shape[2:]), dinv)
    off, diagonal = pl.pallas_call(
        hand_over,
        out_shape=(jax.ShapeDtypeStruct(off.shape, f32), jax.ShapeDtypeStruct(dinv.shape, f32)),
        in_specs=[hbm] * 2,
        out_specs=(hbm, hbm),
        scratch_shapes=[pltpu.VMEM(off.shape, f32), pltpu.VMEM(dinv.shape, f32), dma((2, PIECES)), dma((2,))],
    )(off, diagonal)
    return off.reshape(panel.shape), diagonal


def fits_square_grid(mesh_shape, inverse, panel, pattern, dinv):
    n_row, n_col = mesh_shape["row"], mesh_shape["col"]
    width = inverse.shape[3]
    return (
        n_row == 2 * GRID and n_col == 2
        and inverse.shape[2] == width and width % 128 == 0
        and pattern.shape == (GRID, GRID)
        and panel.shape[2] * GRID == width and panel.shape[3] == GRID * width
        and dinv.shape == (GRID, width // n_row, width // n_col)
    )


def body(inverse, panel, pattern, dinv):
    sizes = {"row": lax.axis_size("row"), "col": lax.axis_size("col")}
    if fits_square_grid(sizes, inverse, panel, pattern, dinv):
        return square_grid(inverse, panel, pattern, dinv)
    return general_body(inverse, panel, pattern, dinv)


def solution(mesh):
    return jax.shard_map(
        body,
        mesh=mesh,
        in_specs=(
            P(("pole", "row"), "col", None, None),
            P(("pole", "row"), "col", None, None),
            P(),
            P("pole", "row", "col"),
        ),
        out_specs=(P(("pole", "row"), "col", None, None), P("pole", "row", "col")),
        check_vma=False,
    )
```

```python
import jax
import jax.numpy as jnp
from jax import lax
from jax.experimental import pallas as pl
from jax.experimental.pallas import tpu as pltpu
from jax.sharding import PartitionSpec as P


def swapped(value, axis, apart):
    mask = 2**apart
    pairs = [(source, source ^ mask) for source in range(lax.axis_size(axis))]
    return lax.ppermute(value, axis, pairs)


def group_flip(current, position, col_bits):
    if position < col_bits:
        return swapped(current, "col", position)
    return swapped(current, "row", position - col_bits)


def cross_flip(current, position, col_bits):
    if position < col_bits:
        return swapped(current, "col", position)
    return swapped(current, "row", position - col_bits)


def bit_at(device_at, position):
    return device_at >> position & 1


def collect(current, positions, device_at, col_bits):
    for position in positions:
        partner = group_flip(current, position, col_bits)
        upper_half = bit_at(device_at, position) == 1
        current = jnp.where(
            upper_half,
            jnp.concatenate([partner, current], 0),
            jnp.concatenate([current, partner], 0),
        )
    return current


def reduce_split(current, positions, device_at, col_bits):
    for position in positions:
        halfway = current.shape[0] // 2
        mine_bit = bit_at(device_at, position)
        kept_half = lax.dynamic_slice_in_dim(current, mine_bit * halfway, halfway, 0)
        sent_half = lax.dynamic_slice_in_dim(current, (1 - mine_bit) * halfway, halfway, 0)
        current = kept_half + group_flip(sent_half, position, col_bits)
    return current


def relabel(current, targets, device_at, col_bits):
    mapping = list(range(len(targets)))
    for column in range(len(targets)):
        if mapping[column] != targets[column]:
            lead_bit = mapping[column]
            other_bit = targets[column]
            shifted = cross_flip(cross_flip(current, lead_bit, col_bits), other_bit, col_bits)
            unequal = bit_at(device_at, lead_bit) != bit_at(device_at, other_bit)
            current = jnp.where(unequal, shifted, current)
            mapping = [
                other_bit if element == lead_bit else lead_bit if element == other_bit else element
                for element in mapping
            ]
    return current


def general_body(inverse, panel, pattern, dinv):
    n_row = lax.axis_size("row")
    n_col = lax.axis_size("col")
    device_at = lax.axis_index("row") * n_col + lax.axis_index("col")
    grid_rows = min(8, n_row // 2)
    grid_cols = n_row * n_col // grid_rows
    col_bits = n_col.bit_length() - 1
    total_bits = (n_row * n_col).bit_length() - 1
    high_bits = grid_rows.bit_length() - 1
    side_bits = total_bits - high_bits
    grid_row = device_at // grid_cols
    grid_col = device_at % grid_cols
    rows_dev, col_count = (panel.shape[2], panel.shape[3])
    nblocks, sup_count = pattern.shape
    sup_width = col_count // sup_count
    first_row = (grid_col * grid_rows + grid_row) * rows_dev
    global_rows = first_row + jnp.arange(rows_dev, dtype=jnp.int32)
    onehot = (
        global_rows[:, None] // sup_width == jnp.arange(nblocks, dtype=jnp.int32)[None, :]
    ).astype(jnp.float32)
    keep_sup = jnp.dot(onehot, pattern.astype(jnp.float32), precision=lax.Precision.HIGHEST)
    keep_piece = jnp.broadcast_to(keep_sup[:, :, None], (rows_dev, sup_count, sup_width)).reshape(
        rows_dev, col_count
    )
    lhat_piece = panel.reshape(rows_dev, col_count) * keep_piece
    inverse_block = inverse.reshape(inverse.shape[2], inverse.shape[3])
    gathered = collect(lhat_piece, list(range(side_bits, total_bits)), device_at, col_bits)
    partial_sum = jnp.dot(
        inverse_block, gathered, precision=lax.Precision.HIGHEST, preferred_element_type=jnp.float32
    )
    row_piece = reduce_split(partial_sum, list(range(side_bits - 1, -1, -1)), device_at, col_bits)
    backward = [(bit_slot + side_bits) % total_bits for bit_slot in range(total_bits)]
    product_piece = relabel(row_piece, backward, device_at, col_bits)
    diag_terms = jnp.einsum(
        "rkw,rkv->kwv",
        lhat_piece.reshape(rows_dev, sup_count, sup_width),
        product_piece.reshape(rows_dev, sup_count, sup_width),
        precision=lax.Precision.HIGHEST,
    )
    arranged = diag_terms.reshape(sup_count, n_row, sup_width // n_row, n_col, sup_width // n_col)
    arranged = arranged.transpose(1, 3, 0, 2, 4).reshape(
        n_row * n_col, sup_count, sup_width // n_row, sup_width // n_col
    )
    diagonal = dinv + lax.psum_scatter(arranged, ("row", "col"), scatter_dimension=0, tiled=True)[0]
    off_diagonal = (-(product_piece * keep_piece)).reshape(panel.shape)
    return (off_diagonal, diagonal)


MESH = pl.DeviceIdType.MESH
HIGHEST = lax.Precision.HIGHEST
GRID = 4
CHUNKS = 4
PIECES = 2

ROUTES = {
    (0, 0): ([(1, 0, 0)], [], [(1, 0, 2)], [(1, 0, 3)]),
    (0, 1): ([(0, 0, 1)], [], [(0, 2, 1)], [(0, 3, 1)]),
    (0, 2): ([(0, 0, 2)], [], [(0, 3, 2)], []),
    (0, 3): ([(0, 0, 3)], [], [], []),
    (1, 0): ([(1, 1, 0)], [(2, 0, 0)], [(1, 2, 0)], [(1, 3, 0)]),
    (1, 1): ([(0, 1, 1), (2, 1, 1)], [(2, 1, 0)], [(0, 1, 2)], [(0, 1, 3)]),
    (1, 2): ([(1, 1, 2)], [(0, 2, 2)], [(0, 2, 3), (1, 3, 2)], []),
    (1, 3): ([(1, 1, 3)], [(0, 3, 3)], [], []),
}

def one(step):
    return [(step, chunk) for chunk in range(CHUNKS)]


def both(chunks):
    return [(step, chunk) for chunk in chunks for step in (1, 2)]


RELAY_AT = (
    {(1, 0): one(0), (1, 1): one(0) + both(range(CHUNKS)), (1, 2): one(0), (0, 0): both(range(CHUNKS))},
    {},
    {(1, 3): one(0)},
    {(0, 2): one(1), (1, 2): one(1)},
    {(1, 0): both(range(CHUNKS)), (0, 1): both(range(CHUNKS))},
    {}, {}, {},
)


def numbered(routes):
    count = 0
    out = []
    for targets in routes:
        out.append([(count + n,) + t for n, t in enumerate(targets)])
        count += len(targets)
    return out


def kernel(pattern_hbm, a_hbm, p_hbm, off_ref, diag_ref,
           pattern_ref, a_ref, l_sem, w_sem, abuf, pbuf, acc, xacc, stage, dpart, dbuf, ebuf,
           a_send, a_recv, p_send, p_recv, f_send, g_send, o_send, o_recv,
           d_send, d_recv, e_send, e_recv):
    width = a_hbm.shape[0]
    sub = p_hbm.shape[0]
    slab = width // CHUNKS
    half_u, half_v = diag_ref.shape[1], diag_ref.shape[2]
    pole = lax.axis_index("pole")
    row = lax.axis_index("row")
    c = lax.axis_index("col")
    z = row // 2
    y = row % 2
    q = 2 * y + c
    mirror = z // 2

    def flip(v):
        return v + mirror * (GRID - 1 - 2 * v)

    zf, qf = flip(z), flip(q)

    def dev(zt, qt):
        return (pole, zt * 2 + qt // 2, qt % 2)

    def copy_to(src, dst, send, recv, where):
        return pltpu.make_async_remote_copy(
            src_ref=src, dst_ref=dst, send_sem=send, recv_sem=recv,
            device_id=where, device_id_type=MESH)

    def cols(k):
        return pl.ds(pl.multiple_of(k * width, width), width)

    def part(block, r):
        return pl.ds(pl.multiple_of(block * width + r * sub, sub), sub)

    loads = [
        pltpu.make_async_copy(pattern_hbm, pattern_ref, l_sem.at[0]),
        pltpu.make_async_copy(p_hbm.at[:, cols(z)], pbuf.at[part(q, z), :], l_sem.at[1]),
        pltpu.make_async_copy(a_hbm, a_ref, l_sem.at[2]),
    ]
    for cp in loads:
        cp.start()

    barrier = pltpu.get_barrier_semaphore()
    for d in range(1, GRID):
        pl.semaphore_signal(barrier, inc=1, device_id=dev(z, (q + d) % GRID), device_id_type=MESH)
        pl.semaphore_signal(barrier, inc=1, device_id=dev((z + d) % GRID, q), device_id_type=MESH)
    pl.semaphore_wait(barrier, 2 * (GRID - 1))

    core_mate = q + 1 - 2 * c
    across = q + 2 - 4 * y

    def a_copy(src, n, tz, tq, slot, chunk):
        rows = pl.ds(chunk * slab, slab)
        return copy_to(src.at[rows, :], abuf.at[flip(slot), rows, :], a_send.at[n * CHUNKS + chunk],
                       a_recv.at[flip(slot) * CHUNKS + chunk], dev(flip(tz), flip(tq)))

    for (cz, cq), routes in ROUTES.items():
        @pl.when((zf == cz) & (qf == cq))
        def _():
            for chunk in range(CHUNKS):
                for n, tz, tq, slot in numbered(routes)[0]:
                    a_copy(a_hbm, n, tz, tq, slot, chunk).start()

    z_copies = []
    for d in (1, 3, 2):
        zt = (z + d) % GRID
        cp = copy_to(p_hbm.at[:, cols(zt)], pbuf.at[part(q, z), :], p_send.at[d], p_recv.at[q * GRID + z], dev(zt, q))
        cp.start()
        z_copies.append(cp)

    upper, odd = qf // 2, qf % 2
    away = 1 - zf
    slots = (
        flip((1 - upper) * away + upper * qf),
        flip((1 - upper) * 2 + upper * ((1 - odd) * 3 + odd * away)),
        flip((1 - upper) * 3 + upper * ((1 - odd) * away + odd * 2)),
    )

    def a_wait(step, chunk):
        slot = slots[step]
        ref = abuf.at[slot, pl.ds(chunk * slab, slab), :]
        pltpu.make_async_copy(ref, ref, a_recv.at[slot * CHUNKS + chunk]).wait()

    def a_relay(place):
        for (cz, cq), routes in ROUTES.items():
            steps = RELAY_AT[place].get((cz, cq), ())
            if steps:
                @pl.when((zf == cz) & (qf == cq))
                def _():
                    for step, chunk in steps:
                        a_wait(step, chunk)
                        for n, tz, tq, slot in numbered(routes)[step + 1]:
                            a_copy(abuf.at[slots[step]], n, tz, tq, slot, chunk).start()

    def a_arrive(step):
        for (cz, cq), routes in ROUTES.items():
            if not routes[step + 1]:
                @pl.when((zf == cz) & (qf == cq))
                def _():
                    for chunk in range(CHUNKS):
                        a_wait(step, chunk)

    def p_wait(block, r):
        ref = pbuf.at[part(block, r), :]
        pltpu.make_async_copy(ref, ref, p_recv.at[block * GRID + r]).wait()

    layer_copies = []

    def p_share(src, r, d):
        for n, qt in ((0, across), (1, core_mate)):
            cp = copy_to(src, pbuf.at[part(q, r), :], f_send.at[2 * d + n], p_recv.at[q * GRID + r], dev(z, qt))
            cp.start()
            layer_copies.append(cp)

    p_share(p_hbm.at[:, cols(z)], z, 0)
    for cp in loads:
        cp.wait()
    a_relay(0)
    for place, d in enumerate((1, 3, 2)):
        r = (z + d) % GRID
        p_wait(q, r)
        p_share(pbuf.at[part(q, r), :], r, d)
        a_relay(place + 1)
    for place, d in enumerate((0, 1, 3, 2)):
        a_relay(4 + place)
        r = (z + d) % GRID
        p_wait(across, r)
        ref = pbuf.at[part(across, r), :]
        cp = copy_to(ref, ref, g_send.at[d], p_recv.at[across * GRID + r], dev(z, core_mate))
        cp.start()
        layer_copies.append(cp)
    for block in (core_mate, core_mate + 2 - 4 * y):
        for r in range(GRID):
            p_wait(block, r)

    def lhat(block):
        rows = pl.ds(pl.multiple_of(block * width, width), width)
        return pbuf[rows, :] * pattern_ref[block, z].astype(jnp.float32)

    def dot_t(left, right):
        return lax.dot_general(left, right, (((0,), (0,)), ((), ())), precision=HIGHEST,
                               preferred_element_type=jnp.float32)

    term_copies = [
        copy_to(dpart.at[(q + d) % GRID], dbuf.at[d - 1], d_send.at[d], d_recv.at[d - 1], dev(z, (q + d) % GRID))
        for d in (2, 1, 3)]

    def send_terms():
        own = lhat(q)
        terms = dot_t(own, xacc[...]) + dot_t(xacc[...], own)
        for zt in range(GRID):
            for qt in range(GRID):
                u, v = zt * sub + (qt // 2) * half_u, (qt % 2) * half_v
                dpart[qt, zt] = terms[u:u + half_u, v:v + half_v]
        for cp in term_copies:
            cp.start()

    first = dot_t(a_ref[...], lhat(z))
    acc[...] = first

    @pl.when(q == z)
    def _():
        xacc[...] = 0.5 * first

    @pl.when(q != z)
    def _():
        xacc[...] = jnp.zeros_like(first)

    for step in range(3):
        a_arrive(step)
        slot = slots[step]
        slot_f = flip(slot)
        turned = (qf != zf) & (qf >= 2) & (slot_f < qf)

        @pl.when(turned)
        def _():
            acc[...] += dot_t(abuf[slot], lhat(slot))

        @pl.when(jnp.logical_not(turned))
        def _():
            more = jnp.dot(abuf[slot], lhat(slot), precision=HIGHEST, preferred_element_type=jnp.float32)
            acc[...] += more

            @pl.when(slot == q)
            def _():
                xacc[...] += 0.5 * more

            @pl.when(slot != q)
            def _():
                xacc[...] += more

        if step < 2:
            @pl.when(qf == 3 - step)
            def _():
                send_terms()


    @pl.when(qf < 2)
    def _():
        send_terms()

    product = acc[...]
    stage[...] = -(product * pattern_ref[q, z].astype(jnp.float32))
    out_copies = []
    for d in (1, 3, 2):
        zt = (z + d) % GRID
        cp = copy_to(stage.at[part(0, zt), :], off_ref.at[:, cols(z)], o_send.at[d], o_recv.at[z], dev(zt, q))
        cp.start()
        out_copies.append(cp)
    out_copies += term_copies
    writes = [pltpu.make_async_copy(stage.at[part(0, z), :], off_ref.at[:, cols(z)], w_sem.at[0])]
    writes[0].start()
    total = dpart[q]
    for d in (1, 2, 3):
        pltpu.make_async_copy(dbuf.at[d - 1], dbuf.at[d - 1], d_recv.at[d - 1]).wait()
        total = total + dbuf[d - 1]
    ebuf[...] = total
    for d in (1, 3, 2):
        zt = (z + d) % GRID
        cp = copy_to(ebuf.at[zt], diag_ref.at[z], e_send.at[d], e_recv.at[z], dev(zt, q))
        cp.start()
        out_copies.append(cp)
    writes.append(pltpu.make_async_copy(ebuf.at[z], diag_ref.at[z], w_sem.at[1]))
    writes[1].start()
    for d in (1, 3, 2):
        k = (z + d) % GRID
        pltpu.make_async_copy(diag_ref.at[k], diag_ref.at[k], e_recv.at[k]).wait()
    for d in (1, 3, 2):
        zs = (z + d) % GRID
        ref = off_ref.at[:, cols(zs)]
        pltpu.make_async_copy(ref, ref, o_recv.at[zs]).wait()
    for cp in writes:
        cp.wait()
    for cp in z_copies + layer_copies + out_copies:
        cp.wait_send()
    for (cz, cq), routes in ROUTES.items():
        @pl.when((zf == cz) & (qf == cq))
        def _():
            for targets in numbered(routes):
                for n, tz, tq, slot in targets:
                    for chunk in range(CHUNKS):
                        a_copy(a_ref, n, tz, tq, slot, chunk).wait_send()


def hand_over(off_in, diag_in, dinv_in, off_out, diag_out, off_held, diag_held, dinv_held, off_sem, diag_sem):
    rows = off_in.shape[0] // PIECES
    pairs = [(
        pltpu.make_async_copy(diag_in, diag_held, diag_sem.at[0]),
        pltpu.make_async_copy(diag_held, diag_out, diag_sem.at[1]),
    )]
    for n in range(PIECES):
        piece = pl.ds(n * rows, rows)
        pairs.append((
            pltpu.make_async_copy(off_in.at[piece, :], off_held.at[piece, :], off_sem.at[0, n]),
            pltpu.make_async_copy(off_held.at[piece, :], off_out.at[piece, :], off_sem.at[1, n]),
        ))
    dinv_load = pltpu.make_async_copy(dinv_in, dinv_held, diag_sem.at[2])
    dinv_load.start()
    for load, store in pairs:
        load.start()
    dinv_load.wait()
    for n, (load, store) in enumerate(pairs):
        load.wait()
        if n == 0:
            diag_held[...] += dinv_held[...]
        store.start()
    for load, store in pairs:
        store.wait()


def square_grid(inverse, panel, pattern, dinv):
    width = inverse.shape[3]
    sub, ncols = panel.shape[2], panel.shape[3]
    hbm = pl.BlockSpec(memory_space=pltpu.HBM)
    dma = pltpu.SemaphoreType.DMA
    f32 = jnp.float32
    off, diagonal = pl.pallas_call(
        kernel,
        out_shape=(jax.ShapeDtypeStruct((sub, ncols), f32), jax.ShapeDtypeStruct(dinv.shape, f32)),
        in_specs=[hbm] * 3,
        out_specs=(hbm, hbm),
        scratch_shapes=[
            pltpu.SMEM(pattern.shape, pattern.dtype),
            pltpu.VMEM((width, width), f32),
            dma((3,)),
            dma((2,)),
            pltpu.VMEM((GRID, width, width), f32),
            pltpu.VMEM((GRID * width, width), f32),
            pltpu.VMEM((width, width), f32),
            pltpu.VMEM((width, width), f32),
            pltpu.VMEM((width, width), f32),
            pltpu.VMEM((GRID,) + dinv.shape, f32),
            pltpu.VMEM((GRID - 1,) + dinv.shape, f32),
            pltpu.VMEM(dinv.shape, f32),
            dma((8 * CHUNKS,)), dma((GRID * CHUNKS,)), dma((GRID,)), dma((GRID * GRID,)), dma((2 * GRID,)), dma((GRID,)),
            dma((GRID,)), dma((GRID,)), dma((GRID,)), dma((GRID,)), dma((GRID,)), dma((GRID,)),
        ],
        compiler_params=pltpu.CompilerParams(
            collective_id=0, has_side_effects=True, vmem_limit_bytes=56 * 1024 * 1024),
    )(pattern, inverse.reshape(inverse.shape[2:]), panel.reshape(panel.shape[2:]))
    off, diagonal = pl.pallas_call(
        hand_over,
        out_shape=(jax.ShapeDtypeStruct(off.shape, f32), jax.ShapeDtypeStruct(dinv.shape, f32)),
        in_specs=[hbm] * 3,
        out_specs=(hbm, hbm),
        scratch_shapes=[pltpu.VMEM(off.shape, f32), pltpu.VMEM(dinv.shape, f32), pltpu.VMEM(dinv.shape, f32),
                        dma((2, PIECES)), dma((3,))],
    )(off, diagonal, dinv)
    return off.reshape(panel.shape), diagonal


def fits_square_grid(mesh_shape, inverse, panel, pattern, dinv):
    n_row, n_col = mesh_shape["row"], mesh_shape["col"]
    width = inverse.shape[3]
    return (
        n_row == 2 * GRID and n_col == 2
        and inverse.shape[2] == width and width % 128 == 0
        and pattern.shape == (GRID, GRID)
        and panel.shape[2] * GRID == width and panel.shape[3] == GRID * width
        and dinv.shape == (GRID, width // n_row, width // n_col)
    )


def body(inverse, panel, pattern, dinv):
    sizes = {"row": lax.axis_size("row"), "col": lax.axis_size("col")}
    if fits_square_grid(sizes, inverse, panel, pattern, dinv):
        return square_grid(inverse, panel, pattern, dinv)
    return general_body(inverse, panel, pattern, dinv)


def solution(mesh):
    return jax.shard_map(
        body,
        mesh=mesh,
        in_specs=(
            P(("pole", "row"), "col", None, None),
            P(("pole", "row"), "col", None, None),
            P(),
            P("pole", "row", "col"),
        ),
        out_specs=(P(("pole", "row"), "col", None, None), P("pole", "row", "col")),
        check_vma=False,
    )
```

```python
import jax
import jax.numpy as jnp
from jax import lax
from jax.experimental import pallas as pl
from jax.experimental.pallas import tpu as pltpu
from jax.sharding import PartitionSpec as P


def swapped(value, axis, apart):
    mask = 2**apart
    pairs = [(source, source ^ mask) for source in range(lax.axis_size(axis))]
    return lax.ppermute(value, axis, pairs)


def group_flip(current, position, col_bits):
    if position < col_bits:
        return swapped(current, "col", position)
    return swapped(current, "row", position - col_bits)


def cross_flip(current, position, col_bits):
    if position < col_bits:
        return swapped(current, "col", position)
    return swapped(current, "row", position - col_bits)


def bit_at(device_at, position):
    return device_at >> position & 1


def collect(current, positions, device_at, col_bits):
    for position in positions:
        partner = group_flip(current, position, col_bits)
        upper_half = bit_at(device_at, position) == 1
        current = jnp.where(
            upper_half,
            jnp.concatenate([partner, current], 0),
            jnp.concatenate([current, partner], 0),
        )
    return current


def reduce_split(current, positions, device_at, col_bits):
    for position in positions:
        halfway = current.shape[0] // 2
        mine_bit = bit_at(device_at, position)
        kept_half = lax.dynamic_slice_in_dim(current, mine_bit * halfway, halfway, 0)
        sent_half = lax.dynamic_slice_in_dim(current, (1 - mine_bit) * halfway, halfway, 0)
        current = kept_half + group_flip(sent_half, position, col_bits)
    return current


def relabel(current, targets, device_at, col_bits):
    mapping = list(range(len(targets)))
    for column in range(len(targets)):
        if mapping[column] != targets[column]:
            lead_bit = mapping[column]
            other_bit = targets[column]
            shifted = cross_flip(cross_flip(current, lead_bit, col_bits), other_bit, col_bits)
            unequal = bit_at(device_at, lead_bit) != bit_at(device_at, other_bit)
            current = jnp.where(unequal, shifted, current)
            mapping = [
                other_bit if element == lead_bit else lead_bit if element == other_bit else element
                for element in mapping
            ]
    return current


def general_body(inverse, panel, pattern, dinv):
    n_row = lax.axis_size("row")
    n_col = lax.axis_size("col")
    device_at = lax.axis_index("row") * n_col + lax.axis_index("col")
    grid_rows = min(8, n_row // 2)
    grid_cols = n_row * n_col // grid_rows
    col_bits = n_col.bit_length() - 1
    total_bits = (n_row * n_col).bit_length() - 1
    high_bits = grid_rows.bit_length() - 1
    side_bits = total_bits - high_bits
    grid_row = device_at // grid_cols
    grid_col = device_at % grid_cols
    rows_dev, col_count = (panel.shape[2], panel.shape[3])
    nblocks, sup_count = pattern.shape
    sup_width = col_count // sup_count
    first_row = (grid_col * grid_rows + grid_row) * rows_dev
    global_rows = first_row + jnp.arange(rows_dev, dtype=jnp.int32)
    onehot = (
        global_rows[:, None] // sup_width == jnp.arange(nblocks, dtype=jnp.int32)[None, :]
    ).astype(jnp.float32)
    keep_sup = jnp.dot(onehot, pattern.astype(jnp.float32), precision=lax.Precision.HIGHEST)
    keep_piece = jnp.broadcast_to(keep_sup[:, :, None], (rows_dev, sup_count, sup_width)).reshape(
        rows_dev, col_count
    )
    lhat_piece = panel.reshape(rows_dev, col_count) * keep_piece
    inverse_block = inverse.reshape(inverse.shape[2], inverse.shape[3])
    gathered = collect(lhat_piece, list(range(side_bits, total_bits)), device_at, col_bits)
    partial_sum = jnp.dot(
        inverse_block, gathered, precision=lax.Precision.HIGHEST, preferred_element_type=jnp.float32
    )
    row_piece = reduce_split(partial_sum, list(range(side_bits - 1, -1, -1)), device_at, col_bits)
    backward = [(bit_slot + side_bits) % total_bits for bit_slot in range(total_bits)]
    product_piece = relabel(row_piece, backward, device_at, col_bits)
    diag_terms = jnp.einsum(
        "rkw,rkv->kwv",
        lhat_piece.reshape(rows_dev, sup_count, sup_width),
        product_piece.reshape(rows_dev, sup_count, sup_width),
        precision=lax.Precision.HIGHEST,
    )
    arranged = diag_terms.reshape(sup_count, n_row, sup_width // n_row, n_col, sup_width // n_col)
    arranged = arranged.transpose(1, 3, 0, 2, 4).reshape(
        n_row * n_col, sup_count, sup_width // n_row, sup_width // n_col
    )
    diagonal = dinv + lax.psum_scatter(arranged, ("row", "col"), scatter_dimension=0, tiled=True)[0]
    off_diagonal = (-(product_piece * keep_piece)).reshape(panel.shape)
    return (off_diagonal, diagonal)


MESH = pl.DeviceIdType.MESH
HIGHEST = lax.Precision.HIGHEST
GRID = 4
CHUNKS = 4
PIECES = 2

ROUTES = {
    (0, 0): ([(1, 0, 0)], [], [(1, 0, 2)], [(1, 0, 3)]),
    (0, 1): ([(0, 0, 1)], [], [(0, 2, 1)], [(0, 3, 1)]),
    (0, 2): ([(0, 0, 2)], [], [(0, 3, 2)], []),
    (0, 3): ([(0, 0, 3)], [], [], []),
    (1, 0): ([(1, 1, 0)], [(2, 0, 0)], [(1, 2, 0)], [(1, 3, 0)]),
    (1, 1): ([(0, 1, 1), (2, 1, 1)], [(2, 1, 0)], [(0, 1, 2)], [(0, 1, 3)]),
    (1, 2): ([(1, 1, 2)], [(0, 2, 2)], [(0, 2, 3), (1, 3, 2)], []),
    (1, 3): ([(1, 1, 3)], [(0, 3, 3)], [], []),
}

def one(step):
    return [(step, chunk) for chunk in range(CHUNKS)]


def both(chunks):
    return [(step, chunk) for chunk in chunks for step in (1, 2)]


RELAY_AT = (
    {(1, 0): one(0), (1, 1): one(0) + both(range(CHUNKS)), (1, 2): one(0), (0, 0): both(range(CHUNKS))},
    {},
    {(1, 3): one(0)},
    {(0, 2): one(1), (1, 2): one(1)},
    {(1, 0): both(range(CHUNKS)), (0, 1): both(range(CHUNKS))},
    {}, {}, {},
)


def numbered(routes):
    count = 0
    out = []
    for targets in routes:
        out.append([(count + n,) + t for n, t in enumerate(targets)])
        count += len(targets)
    return out


def kernel(pattern_hbm, a_hbm, p_hbm, off_ref, diag_ref,
           pattern_ref, a_ref, l_sem, w_sem, abuf, pbuf, acc, xacc, stage, dpart, dbuf, ebuf,
           a_send, a_recv, p_send, p_recv, f_send, g_send, o_send, o_recv,
           d_send, d_recv, e_send, e_recv):
    width = a_hbm.shape[0]
    sub = p_hbm.shape[0]
    slab = width // CHUNKS
    half_u, half_v = diag_ref.shape[1], diag_ref.shape[2]
    pole = lax.axis_index("pole")
    row = lax.axis_index("row")
    c = lax.axis_index("col")
    z = row // 2
    y = row % 2
    q = 2 * y + c
    mirror = z // 2

    def flip(v):
        return v + mirror * (GRID - 1 - 2 * v)

    zf, qf = flip(z), flip(q)

    def dev(zt, qt):
        return (pole, zt * 2 + qt // 2, qt % 2)

    def copy_to(src, dst, send, recv, where):
        return pltpu.make_async_remote_copy(
            src_ref=src, dst_ref=dst, send_sem=send, recv_sem=recv,
            device_id=where, device_id_type=MESH)

    def cols(k):
        return pl.ds(pl.multiple_of(k * width, width), width)

    def part(block, r):
        return pl.ds(pl.multiple_of(block * width + r * sub, sub), sub)

    loads = [
        pltpu.make_async_copy(pattern_hbm, pattern_ref, l_sem.at[0]),
        pltpu.make_async_copy(p_hbm.at[:, cols(z)], pbuf.at[part(q, z), :], l_sem.at[1]),
        pltpu.make_async_copy(a_hbm, a_ref, l_sem.at[2]),
    ]
    for cp in loads:
        cp.start()

    barrier = pltpu.get_barrier_semaphore()
    for d in range(1, GRID):
        pl.semaphore_signal(barrier, inc=1, device_id=dev(z, (q + d) % GRID), device_id_type=MESH)
        pl.semaphore_signal(barrier, inc=1, device_id=dev((z + d) % GRID, q), device_id_type=MESH)
    pl.semaphore_wait(barrier, 2 * (GRID - 1))

    core_mate = q + 1 - 2 * c
    across = q + 2 - 4 * y

    def a_copy(src, n, tz, tq, slot, chunk):
        rows = pl.ds(chunk * slab, slab)
        return copy_to(src.at[rows, :], abuf.at[flip(slot), rows, :], a_send.at[n * CHUNKS + chunk],
                       a_recv.at[flip(slot) * CHUNKS + chunk], dev(flip(tz), flip(tq)))

    for (cz, cq), routes in ROUTES.items():
        @pl.when((zf == cz) & (qf == cq))
        def _():
            for chunk in range(CHUNKS):
                for n, tz, tq, slot in numbered(routes)[0]:
                    a_copy(a_hbm, n, tz, tq, slot, chunk).start()

    z_copies = []
    for d in (1, 3, 2):
        zt = (z + d) % GRID
        cp = copy_to(p_hbm.at[:, cols(zt)], pbuf.at[part(q, z), :], p_send.at[d], p_recv.at[q * GRID + z], dev(zt, q))
        cp.start()
        z_copies.append(cp)

    upper, odd = qf // 2, qf % 2
    away = 1 - zf
    slots = (
        flip((1 - upper) * away + upper * qf),
        flip((1 - upper) * 2 + upper * ((1 - odd) * 3 + odd * away)),
        flip((1 - upper) * 3 + upper * ((1 - odd) * away + odd * 2)),
    )

    def a_wait(step, chunk):
        slot = slots[step]
        ref = abuf.at[slot, pl.ds(chunk * slab, slab), :]
        pltpu.make_async_copy(ref, ref, a_recv.at[slot * CHUNKS + chunk]).wait()

    def a_relay(place):
        for (cz, cq), routes in ROUTES.items():
            steps = RELAY_AT[place].get((cz, cq), ())
            if steps:
                @pl.when((zf == cz) & (qf == cq))
                def _():
                    for step, chunk in steps:
                        a_wait(step, chunk)
                        for n, tz, tq, slot in numbered(routes)[step + 1]:
                            a_copy(abuf.at[slots[step]], n, tz, tq, slot, chunk).start()

    def a_arrive(step):
        for (cz, cq), routes in ROUTES.items():
            if not routes[step + 1]:
                @pl.when((zf == cz) & (qf == cq))
                def _():
                    for chunk in range(CHUNKS):
                        a_wait(step, chunk)

    def p_wait(block, r):
        ref = pbuf.at[part(block, r), :]
        pltpu.make_async_copy(ref, ref, p_recv.at[block * GRID + r]).wait()

    layer_copies = []

    def p_share(src, r, d):
        for n, qt in ((0, across), (1, core_mate)):
            cp = copy_to(src, pbuf.at[part(q, r), :], f_send.at[2 * d + n], p_recv.at[q * GRID + r], dev(z, qt))
            cp.start()
            layer_copies.append(cp)

    p_share(p_hbm.at[:, cols(z)], z, 0)
    for cp in loads:
        cp.wait()
    a_relay(0)
    for place, d in enumerate((1, 3, 2)):
        r = (z + d) % GRID
        p_wait(q, r)
        p_share(pbuf.at[part(q, r), :], r, d)
        a_relay(place + 1)
    for place, d in enumerate((0, 1, 3, 2)):
        a_relay(4 + place)
        r = (z + d) % GRID
        p_wait(across, r)
        ref = pbuf.at[part(across, r), :]
        cp = copy_to(ref, ref, g_send.at[d], p_recv.at[across * GRID + r], dev(z, core_mate))
        cp.start()
        layer_copies.append(cp)
    for block in (core_mate, core_mate + 2 - 4 * y):
        for r in range(GRID):
            p_wait(block, r)

    def lhat(block):
        rows = pl.ds(pl.multiple_of(block * width, width), width)
        return pbuf[rows, :] * pattern_ref[block, z].astype(jnp.float32)

    def dot_t(left, right):
        return lax.dot_general(left, right, (((0,), (0,)), ((), ())), precision=HIGHEST,
                               preferred_element_type=jnp.float32)

    term_copies = [
        copy_to(dpart.at[(q + d) % GRID], dbuf.at[d - 1], d_send.at[d], d_recv.at[d - 1], dev(z, (q + d) % GRID))
        for d in (2, 1, 3)]

    def send_terms():
        own = lhat(q)
        terms = dot_t(own, xacc[...])
        terms = terms + terms.T
        for zt in range(GRID):
            for qt in range(GRID):
                u, v = zt * sub + (qt // 2) * half_u, (qt % 2) * half_v
                dpart[qt, zt] = terms[u:u + half_u, v:v + half_v]
        for cp in term_copies:
            cp.start()

    first = dot_t(a_ref[...], lhat(z))
    acc[...] = first

    @pl.when(q == z)
    def _():
        xacc[...] = 0.5 * first

    @pl.when(q != z)
    def _():
        xacc[...] = jnp.zeros_like(first)

    for step in range(3):
        a_arrive(step)
        slot = slots[step]
        slot_f = flip(slot)
        turned = (qf != zf) & (qf >= 2) & (slot_f < qf)

        @pl.when(turned)
        def _():
            acc[...] += dot_t(abuf[slot], lhat(slot))

        @pl.when(jnp.logical_not(turned))
        def _():
            more = jnp.dot(abuf[slot], lhat(slot), precision=HIGHEST, preferred_element_type=jnp.float32)
            acc[...] += more

            @pl.when(slot == q)
            def _():
                xacc[...] += 0.5 * more

            @pl.when(slot != q)
            def _():
                xacc[...] += more

        if step < 2:
            @pl.when(qf == 3 - step)
            def _():
                send_terms()


    @pl.when(qf < 2)
    def _():
        send_terms()

    product = acc[...]
    stage[...] = -(product * pattern_ref[q, z].astype(jnp.float32))
    out_copies = []
    for d in (1, 3, 2):
        zt = (z + d) % GRID
        cp = copy_to(stage.at[part(0, zt), :], off_ref.at[:, cols(z)], o_send.at[d], o_recv.at[z], dev(zt, q))
        cp.start()
        out_copies.append(cp)
    out_copies += term_copies
    writes = [pltpu.make_async_copy(stage.at[part(0, z), :], off_ref.at[:, cols(z)], w_sem.at[0])]
    writes[0].start()
    total = dpart[q]
    for d in (1, 2, 3):
        pltpu.make_async_copy(dbuf.at[d - 1], dbuf.at[d - 1], d_recv.at[d - 1]).wait()
        total = total + dbuf[d - 1]
    ebuf[...] = total
    for d in (1, 3, 2):
        zt = (z + d) % GRID
        cp = copy_to(ebuf.at[zt], diag_ref.at[z], e_send.at[d], e_recv.at[z], dev(zt, q))
        cp.start()
        out_copies.append(cp)
    writes.append(pltpu.make_async_copy(ebuf.at[z], diag_ref.at[z], w_sem.at[1]))
    writes[1].start()
    for d in (1, 3, 2):
        k = (z + d) % GRID
        pltpu.make_async_copy(diag_ref.at[k], diag_ref.at[k], e_recv.at[k]).wait()
    for d in (1, 3, 2):
        zs = (z + d) % GRID
        ref = off_ref.at[:, cols(zs)]
        pltpu.make_async_copy(ref, ref, o_recv.at[zs]).wait()
    for cp in writes:
        cp.wait()
    for cp in z_copies + layer_copies + out_copies:
        cp.wait_send()
    for (cz, cq), routes in ROUTES.items():
        @pl.when((zf == cz) & (qf == cq))
        def _():
            for targets in numbered(routes):
                for n, tz, tq, slot in targets:
                    for chunk in range(CHUNKS):
                        a_copy(a_ref, n, tz, tq, slot, chunk).wait_send()


def hand_over(off_in, diag_in, dinv_in, off_out, diag_out, off_held, diag_held, dinv_held, off_sem, diag_sem):
    rows = off_in.shape[0] // PIECES
    pairs = [(
        pltpu.make_async_copy(diag_in, diag_held, diag_sem.at[0]),
        pltpu.make_async_copy(diag_held, diag_out, diag_sem.at[1]),
    )]
    for n in range(PIECES):
        piece = pl.ds(n * rows, rows)
        pairs.append((
            pltpu.make_async_copy(off_in.at[piece, :], off_held.at[piece, :], off_sem.at[0, n]),
            pltpu.make_async_copy(off_held.at[piece, :], off_out.at[piece, :], off_sem.at[1, n]),
        ))
    dinv_load = pltpu.make_async_copy(dinv_in, dinv_held, diag_sem.at[2])
    dinv_load.start()
    for load, store in pairs:
        load.start()
    dinv_load.wait()
    for n, (load, store) in enumerate(pairs):
        load.wait()
        if n == 0:
            diag_held[...] += dinv_held[...]
        store.start()
    for load, store in pairs:
        store.wait()


def square_grid(inverse, panel, pattern, dinv):
    width = inverse.shape[3]
    sub, ncols = panel.shape[2], panel.shape[3]
    hbm = pl.BlockSpec(memory_space=pltpu.HBM)
    dma = pltpu.SemaphoreType.DMA
    f32 = jnp.float32
    off, diagonal = pl.pallas_call(
        kernel,
        out_shape=(jax.ShapeDtypeStruct((sub, ncols), f32), jax.ShapeDtypeStruct(dinv.shape, f32)),
        in_specs=[hbm] * 3,
        out_specs=(hbm, hbm),
        scratch_shapes=[
            pltpu.SMEM(pattern.shape, pattern.dtype),
            pltpu.VMEM((width, width), f32),
            dma((3,)),
            dma((2,)),
            pltpu.VMEM((GRID, width, width), f32),
            pltpu.VMEM((GRID * width, width), f32),
            pltpu.VMEM((width, width), f32),
            pltpu.VMEM((width, width), f32),
            pltpu.VMEM((width, width), f32),
            pltpu.VMEM((GRID,) + dinv.shape, f32),
            pltpu.VMEM((GRID - 1,) + dinv.shape, f32),
            pltpu.VMEM(dinv.shape, f32),
            dma((8 * CHUNKS,)), dma((GRID * CHUNKS,)), dma((GRID,)), dma((GRID * GRID,)), dma((2 * GRID,)), dma((GRID,)),
            dma((GRID,)), dma((GRID,)), dma((GRID,)), dma((GRID,)), dma((GRID,)), dma((GRID,)),
        ],
        compiler_params=pltpu.CompilerParams(
            collective_id=0, has_side_effects=True, vmem_limit_bytes=56 * 1024 * 1024),
    )(pattern, inverse.reshape(inverse.shape[2:]), panel.reshape(panel.shape[2:]))
    off, diagonal = pl.pallas_call(
        hand_over,
        out_shape=(jax.ShapeDtypeStruct(off.shape, f32), jax.ShapeDtypeStruct(dinv.shape, f32)),
        in_specs=[hbm] * 3,
        out_specs=(hbm, hbm),
        scratch_shapes=[pltpu.VMEM(off.shape, f32), pltpu.VMEM(dinv.shape, f32), pltpu.VMEM(dinv.shape, f32),
                        dma((2, PIECES)), dma((3,))],
    )(off, diagonal, dinv)
    return off.reshape(panel.shape), diagonal


def fits_square_grid(mesh_shape, inverse, panel, pattern, dinv):
    n_row, n_col = mesh_shape["row"], mesh_shape["col"]
    width = inverse.shape[3]
    return (
        n_row == 2 * GRID and n_col == 2
        and inverse.shape[2] == width and width % 128 == 0
        and pattern.shape == (GRID, GRID)
        and panel.shape[2] * GRID == width and panel.shape[3] == GRID * width
        and dinv.shape == (GRID, width // n_row, width // n_col)
    )


def body(inverse, panel, pattern, dinv):
    sizes = {"row": lax.axis_size("row"), "col": lax.axis_size("col")}
    if fits_square_grid(sizes, inverse, panel, pattern, dinv):
        return square_grid(inverse, panel, pattern, dinv)
    return general_body(inverse, panel, pattern, dinv)


def solution(mesh):
    return jax.shard_map(
        body,
        mesh=mesh,
        in_specs=(
            P(("pole", "row"), "col", None, None),
            P(("pole", "row"), "col", None, None),
            P(),
            P("pole", "row", "col"),
        ),
        out_specs=(P(("pole", "row"), "col", None, None), P("pole", "row", "col")),
        check_vma=False,
    )
```
